32 devices in a mesh: row: 8 (over z, x), col: 4 (over y, core).
Axes of the slice: x: 2, y: 2, z: 4, core: 2. Of those that a mesh axis runs over, the one named last changes fastest.
Arguments:
- volt_start: float32 [2, 256, 1024], P(None, 'row', 'col'), may hold values from 0.6 to 1.2
- cap_dt: float32 [2, 256, 1024], P(None, 'row', 'col'), may hold values from 0.1 to 1
- wire_cond: float32 [2, 256, 1024], P(None, 'row', 'col'), may hold values from 0.5 to 2
- via_cond: float32 [256, 1024], P('row', 'col'), may hold values from 0.2 to 2
- load_current: float32 [256, 1024], P('row', 'col'), may hold values from 0.05 to 0.5
- load_wave: float32 [1], replicated, may hold values from 0.5 to 1.5
- decap_state: float32 [256, 1024], P('row', 'col'), may hold values from 0.6 to 1.2
- decap_cond: float32 [256, 1024], P('row', 'col'), may hold values from 0.1 to 2
- bump_map: int32 [256, 1024], P('row', 'col'), may hold values from 0 to 8191, as said below
- via_mask: int32 [256, 1024], P('row', 'col'), may hold values 0 or 1
- bump_cond: float32 [8192], replicated, may hold values from 0.4 to 0.8
- bump_supply: float32 [8192], replicated, may hold values from 0.5 to 1.5
- package: float32 [8192, 8192], P(('row', 'col')), may hold values from -0.0625 to 0.0625, as said below
Outputs:
- voltage: float32 [2, 256, 1024], P(None, 'row', 'col')
- decap_volt: float32 [256, 1024], P('row', 'col')
- bump_volt: float32 [8192], P(('row', 'col'))
The draws below stay inside these ranges and needn't reach their ends.
Inputs may be any that keep to these rules, and one draw needn't show every extreme that they name: bump_map[i, j] = min((i + s) // 2, 127) * 64 + j // 16, with an integer s drawn for each node, 0 <= s <= 256 / 128 / 4. package is symmetric.
All inputs are finite; a program needn't handle non-finite values. No bound on the sum of `via_mask` on one device may be relied on, other than what follows from the above.
Results may differ from the reference program's by a relative error of at most 0.0001.
Values sent between devices are 32-bit elements; how exact they have to be, the bound alone decides.
No kernel may reach another device: no remote copies, remote signals or barrier semaphores. Data moves between devices by JAX's collectives and lax.ppermute only.
A program may use at most 64 MiB of HBM per device.

```python
import math
import jax
import jax.numpy as jnp
from jax import lax

BR = 128
BC = 64
DEG = 4
STEPS = 1
B = 8192
NX = 256
NY = 1024


def draw_bump_map(key, part):
    tile_rows = NX // BR
    tile_cols = NY // BC
    reach_rows = max(1, tile_rows // 4)
    jitter = jax.random.randint(jax.random.fold_in(key, 3), (NX, NY), 0, reach_rows + 1)
    row_ids = jnp.arange(NX, dtype=jnp.int32)[:, None]
    col_ids = jnp.arange(NY, dtype=jnp.int32)[None, :]
    lattice_row = jnp.minimum((row_ids + jitter) // tile_rows, BR - 1)
    return (lattice_row * BC + col_ids // tile_cols).astype(jnp.int32)


def draw_package(key, part):
    base_key = jax.random.fold_in(key, 7)
    diag_key, off_key = jax.random.split(base_key)
    diag_part = jax.random.uniform(diag_key, (B,), jnp.float32, 0.6, 1.0)
    noise_draw = jnp.clip(jax.random.normal(off_key, (B, B), jnp.float32), -4.0, 4.0)
    off_part = (noise_draw + noise_draw.T) * (0.15 / math.sqrt(B))
    identity = (jnp.arange(B)[:, None] == jnp.arange(B)[None, :]).astype(jnp.float32)
    scaled = (off_part * (1.0 - identity) + identity * diag_part[None, :]) * (1.6 / (NX * NY // B))
    return scaled.astype(jnp.float32)


def with_ends(array, stream_key, smallest, top_value):
    shape = array.shape
    spot = [jax.random.randint(jax.random.fold_in(stream_key, axis), (), 0, shape[axis]) for axis in range(len(shape))]
    array = array.at[tuple(spot)].set(smallest)
    longest = shape.index(max(shape))
    spot[longest] = (spot[longest] + 1) % shape[longest]
    return array.at[tuple(spot)].set(top_value)


def steps_of(key, dims, cuts, smallest, largest):
    loudness = 1.0
    for axis_at, blocks in cuts:
        heights = jax.random.uniform(jax.random.fold_in(jax.random.fold_in(key, 6), axis_at), (blocks,), jnp.float32, smallest / len(cuts), largest / len(cuts))
        loudness = loudness * jnp.repeat(jnp.exp(heights), dims[axis_at] // blocks).reshape((-1,) + (1,) * (len(dims) - 1 - axis_at))
    return loudness


def setup_inputs(seed: int = 0) -> dict:
    arg_keys = jax.random.split(jax.random.key(seed), 14)
    volt_start = jnp.clip(0.6 + 0.6 * jax.random.uniform(arg_keys[0], (2, NX, NY), jnp.float32) ** steps_of(arg_keys[0], (2, NX, NY), ((1, 8), (2, 4)), -0.2, 0.2), 0.6, 1.2)
    cap_dt = jnp.clip(jnp.exp(math.log(1.0) - 2.3025851 * jax.random.uniform(arg_keys[1], (2, NX, NY), jnp.float32) ** steps_of(arg_keys[1], (2, NX, NY), ((1, 8), (2, 4)), -0.2, 0.2)), 0.1, 1.0)
    wire_cond = jnp.clip(jnp.exp(math.log(2.0) - 1.3862944 * jax.random.uniform(arg_keys[2], (2, NX, NY), jnp.float32) ** steps_of(arg_keys[2], (2, NX, NY), ((1, 8), (2, 4)), -0.2, 0.2)), 0.5, 2.0)
    via_cond = jnp.clip(jnp.exp(math.log(2.0) - 2.3025851 * jax.random.uniform(arg_keys[3], (NX, NY), jnp.float32) ** steps_of(arg_keys[3], (NX, NY), ((0, 8), (1, 4)), -0.2, 0.2)), 0.2, 2.0)
    load_current = jnp.clip(jnp.exp(math.log(0.5) - 2.3025851 * jax.random.uniform(arg_keys[4], (NX, NY), jnp.float32) ** steps_of(arg_keys[4], (NX, NY), ((0, 8), (1, 4)), -0.2, 0.2)), 0.05, 0.5)
    load_wave = jnp.clip(jax.random.uniform(arg_keys[5], (STEPS,), jnp.float32, 0.5, 1.5), 0.5, 1.5)
    decap_state = jnp.clip(0.6 + 0.6 * jax.random.uniform(arg_keys[6], (NX, NY), jnp.float32) ** steps_of(arg_keys[6], (NX, NY), ((0, 8), (1, 4)), -0.2, 0.2), 0.6, 1.2)
    decap_cond = jnp.clip(jnp.exp(math.log(2.0) - 2.9957323 * jax.random.uniform(arg_keys[7], (NX, NY), jnp.float32) ** steps_of(arg_keys[7], (NX, NY), ((0, 8), (1, 4)), -0.2, 0.2)), 0.1, 2.0)
    bump_map = draw_bump_map(jax.random.fold_in(arg_keys[13], 71), 0)
    via_mask = with_ends((jax.random.randint(arg_keys[9], (NX, NY), 0, 2) < 1).astype(jnp.int32), jax.random.fold_in(arg_keys[9], 1), 0, 1)
    bump_cond = jnp.clip(jnp.exp(jax.random.uniform(arg_keys[10], (B,), jnp.float32, math.log(0.4), math.log(0.8))), 0.4, 0.8)
    bump_supply = jnp.clip(jax.random.uniform(arg_keys[11], (B,), jnp.float32, 0.5, 1.5), 0.5, 1.5)
    package = draw_package(jax.random.fold_in(arg_keys[13], 71), 0)
    return dict(volt_start=volt_start, cap_dt=cap_dt, wire_cond=wire_cond, via_cond=via_cond, load_current=load_current, load_wave=load_wave, decap_state=decap_state, decap_cond=decap_cond, bump_map=bump_map, via_mask=via_mask, bump_cond=bump_cond, bump_supply=bump_supply, package=package)


CHEB_LO = 0.05
CHEB_HI = 2.0
CHEB_MID = (CHEB_HI + CHEB_LO) / 2.0
CHEB_HALF = (CHEB_HI - CHEB_LO) / 2.0
CHEB_RATIO = CHEB_MID / CHEB_HALF


def shift_down(values):
    return jnp.pad(values, ((1, 0), (0, 0)))[:-1, :]


def shift_right(values):
    return jnp.pad(values, ((0, 0), (1, 0)))[:, :-1]


def chebyshev(iterate, source, diagonal, apply_matrix):
    residual = source - apply_matrix(iterate)
    direction = residual / (CHEB_MID * diagonal)
    rho_now = 1.0 / CHEB_RATIO
    for sweep in range(DEG):
        iterate = iterate + direction
        if sweep < DEG - 1:
            residual = residual - apply_matrix(direction)
            rho_next = 1.0 / (2.0 * CHEB_RATIO - rho_now)
            direction = rho_next * rho_now * direction + (2.0 * rho_next / CHEB_HALF) * residual / diagonal
            rho_now = rho_next
    return iterate


def reference(volt_start, cap_dt, wire_cond, via_cond, load_current, load_wave, decap_state, decap_cond, bump_map, via_mask, bump_cond, bump_supply, package):
    zero_col = jnp.zeros((NX, 1), jnp.float32).astype(wire_cond.dtype)
    zero_row = jnp.zeros((1, NY), jnp.float32).astype(wire_cond.dtype)
    link_row = jnp.concatenate([wire_cond[0][:, :-1], zero_col], axis=1)
    link_col = jnp.concatenate([wire_cond[1][:-1, :], zero_row], axis=0)
    left_link = shift_right(link_row)
    up_link = shift_down(link_col)
    flat_map = bump_map.reshape(-1)
    node_cond = via_mask.astype(wire_cond.dtype) * jnp.take(bump_cond, bump_map)
    supply_node = node_cond * jnp.take(bump_supply, bump_map)
    decap_frac = decap_cond / (1.0 + decap_cond)
    diag_top = cap_dt[0] + link_row + left_link + via_cond + node_cond
    diag_low = cap_dt[1] + link_col + up_link + via_cond + decap_frac
    diagonal = jnp.stack([diag_top, diag_low])

    def bump_sum(top_layer):
        return jax.ops.segment_sum((node_cond * top_layer).reshape(-1), flat_map, num_segments=B)

    def operate(iterate):
        top_layer = iterate[0]
        low_layer = iterate[1]
        coupled = jnp.dot(package, bump_sum(top_layer), precision=lax.Precision.HIGHEST)
        right_cells = jnp.pad(top_layer, ((0, 0), (0, 1)))[:, 1:]
        left_cells = shift_right(top_layer)
        down_cells = jnp.pad(low_layer, ((0, 1), (0, 0)))[1:, :]
        up_cells = shift_down(low_layer)
        top_out = diag_top * top_layer - link_row * right_cells - left_link * left_cells - via_cond * low_layer - node_cond * jnp.take(coupled, bump_map)
        low_out = diag_low * low_layer - link_col * down_cells - up_link * up_cells - via_cond * top_layer
        return jnp.stack([top_out, low_out])

    voltage = volt_start
    decap_volt = decap_state
    for section in range(STEPS):
        source = jnp.stack([cap_dt[0] * voltage[0] + supply_node, cap_dt[1] * voltage[1] + decap_frac * decap_volt - load_wave[section] * load_current])
        voltage = chebyshev(voltage, source, diagonal, operate)
        decap_volt = (decap_volt + decap_cond * voltage[1]) / (1.0 + decap_cond)
    bump_volt = bump_supply + jnp.dot(package, bump_sum(voltage[0]), precision=lax.Precision.HIGHEST)
    return voltage, decap_volt, bump_volt
```

```python
import collections
import functools

import jax
import jax.numpy as jnp
from jax import lax
from jax.experimental import pallas as pl
from jax.experimental.pallas import tpu as pltpu
from jax.sharding import PartitionSpec as P

BR = 128
BC = 64
DEG = 4

CHEB_LO = 0.05
CHEB_HI = 2.0
CHEB_MID = (CHEB_HI + CHEB_LO) / 2.0
CHEB_HALF = (CHEB_HI - CHEB_LO) / 2.0
CHEB_RATIO = CHEB_MID / CHEB_HALF

LANES = 128
SUBS = 8
AXES = ("row", "col")

Y_ROW = 0
PIECE_ROW = 2
SPILL_ROW = 4
HALO_ROW = 5
REL_ROW = 7
SECOND = 8

(LINK_R, LINK_L, LINK_D, LINK_U, VIA, WEIGHT, DIAG_T, DIAG_B, INV_T, INV_B) = range(10)

Geometry = collections.namedtuple(
    "Geometry",
    [
        "height",
        "breadth",
        "rows",
        "cols",
        "own",
        "block_rows",
        "block_cols",
        "tile_rows",
        "tile_cols",
        "lattice",
    ],
)


def steps_of():
    factors = [(0.0, 1.0 / CHEB_MID)]
    rho_now = 1.0 / CHEB_RATIO
    for _ in range(DEG - 1):
        rho_next = 1.0 / (2.0 * CHEB_RATIO - rho_now)
        factors.append((rho_next * rho_now, 2.0 * rho_next / CHEB_HALF))
        rho_now = rho_next
    return factors


def iota(shape, dim):
    return lax.broadcasted_iota(jnp.int32, shape, dim)


def lookup(table, index):
    return jnp.take_along_axis(table, index, axis=1, mode="promise_in_bounds")


def place():
    row = lax.axis_index("row")
    col = lax.axis_index("col")
    return row, col


def neighbours(geo, row, col):
    me = row * geo.cols + col
    east = jnp.where(col < geo.cols - 1, me + 1, me)
    west = jnp.where(col > 0, me - 1, me)
    south = jnp.where(row < geo.rows - 1, me + geo.cols, me)
    north = jnp.where(row > 0, me - geo.cols, me)
    return me, east, west, south, north


def per_band(geo):
    return geo.block_rows * BC // LANES


def spread(geo, ref, row, col, rel, tiles):
    span = per_band(geo)
    base = row * span
    count = geo.lattice // LANES
    lines = [ref[pl.ds(base + t, 1), :] for t in range(span)]
    lines.append(ref[pl.ds(jnp.minimum(base + span, count - 1), 1), :])
    per_line = LANES // BC
    sub = iota((SUBS, LANES), 0)
    lane = iota((SUBS, LANES), 1)
    last = geo.breadth // LANES
    columns = []
    for q in range(tiles):
        if q < last:
            columns.append(col * geo.block_cols + (lane + q * LANES) // geo.tile_cols)
        else:
            after = jnp.minimum((col + 1) * geo.block_cols, BC - 1)
            before = jnp.maximum(col * geo.block_cols - 1, 0)
            columns.append(jnp.where(lane < LANES // 2, after, before))
    bands = []
    for g in range(geo.height // SUBS):
        picks = []
        for shift in (0, 1):
            levels = [(g * SUBS + i) // geo.tile_rows + shift for i in range(SUBS)]
            held = [level // per_line for level in levels]
            table = jnp.broadcast_to(lines[held[0]], (SUBS, LANES))
            for i in range(1, SUBS):
                if held[i] != held[i - 1]:
                    table = jnp.where(
                        sub >= i, jnp.broadcast_to(lines[held[i]], (SUBS, LANES)), table
                    )
            part = ((g * SUBS + sub) // geo.tile_rows + shift) % per_line
            picks.append([lookup(table, part * BC + columns[q]) for q in range(tiles)])
        bands.append(
            jnp.concatenate(
                [
                    jnp.where(
                        rel[g * SUBS : (g + 1) * SUBS, q * LANES : (q + 1) * LANES] == 0,
                        picks[0][q],
                        picks[1][q],
                    )
                    for q in range(tiles)
                ],
                axis=1,
            )
        )
    return jnp.concatenate(bands, axis=0)


def shares(geo, weighted, rel, col):
    height, breadth = geo.height, geo.breadth
    near = jnp.where(rel == 0, weighted, 0.0)
    both = jnp.concatenate([near, weighted - near], axis=0)
    high = both.astype(jnp.bfloat16)
    rest = both - high.astype(jnp.float32)
    mid = rest.astype(jnp.bfloat16)
    low = (rest - mid.astype(jnp.float32)).astype(jnp.bfloat16)
    adder = (
        iota((breadth, LANES), 0) // geo.tile_cols == iota((breadth, LANES), 1) % geo.block_cols
    )
    adder = adder.astype(jnp.float32).astype(jnp.bfloat16)
    summed = jnp.dot(
        jnp.concatenate([high, mid, low], axis=0), adder, preferred_element_type=jnp.float32
    )
    summed = summed[: 2 * height] + summed[2 * height : 4 * height] + summed[4 * height :]
    sub = iota((SUBS, LANES), 0)
    segment = iota((SUBS, LANES), 1) // geo.block_cols
    segments = LANES // geo.block_cols
    packed = -(-geo.block_rows // segments)
    totals = [jnp.zeros((SUBS, LANES), jnp.float32) for _ in range(packed)]
    spill = jnp.zeros((SUBS, LANES), jnp.float32)
    for shift in (0, 1):
        for g in range(height // SUBS):
            first = g * SUBS // geo.tile_rows + shift
            final = (g * SUBS + SUBS - 1) // geo.tile_rows + shift
            level = (g * SUBS + sub) // geo.tile_rows + shift
            start = shift * height + g * SUBS
            block = summed[start : start + SUBS]
            for h in range(packed):
                if first < (h + 1) * segments and final >= h * segments:
                    hit = level == segment + h * segments
                    if final >= geo.block_rows:
                        hit = hit & (level < geo.block_rows)
                    totals[h] = totals[h] + jnp.where(hit, block, 0.0)
            if final >= geo.block_rows:
                hit = (level == geo.block_rows) & (segment == col)
                spill = spill + jnp.where(hit, block, 0.0)
    lines = [jnp.sum(total, axis=0, keepdims=True) for total in totals]
    return lines, jnp.sum(spill, axis=0, keepdims=True)


def gather_shares(geo, message, offset, out_ref):
    span = per_band(geo)
    per_line = LANES // BC
    segments = LANES // geo.block_cols
    sub = iota((SUBS, LANES), 0)
    lane = iota((SUBS, LANES), 1)
    level = sub * per_line + lane // BC
    index = (level % segments) * geo.block_cols + lane % geo.block_cols
    owner = (lane % BC) // geo.block_cols
    packed = -(-geo.block_rows // segments)

    def band(r):
        total = jnp.zeros((SUBS, LANES), jnp.float32)
        for c in range(geo.cols):
            sender = r * geo.cols + c
            table = jnp.broadcast_to(message[sender, pl.ds(offset + PIECE_ROW, 1), :], (SUBS, LANES))
            for h in range(1, packed):
                line = message[sender, pl.ds(offset + PIECE_ROW + h, 1), :]
                table = jnp.where(
                    sub >= h * segments // per_line, jnp.broadcast_to(line, (SUBS, LANES)), table
                )
            total = jnp.where(owner == c, lookup(table, index), total)
        return total

    def spill(r):
        line = message[r * geo.cols, pl.ds(offset + SPILL_ROW, 1), :]
        for c in range(1, geo.cols):
            line = line + message[r * geo.cols + c, pl.ds(offset + SPILL_ROW, 1), :]
        return jnp.where(sub == 0, jnp.broadcast_to(line, (SUBS, LANES)), 0.0)

    if geo.rows <= 8:
        for r in range(geo.rows):
            total = band(r)
            if r > 0:
                total = total + spill(r - 1)
            out_ref[pl.ds(r * span, span), :] = total[:span]
    else:

        def one(r, carry):
            above = jnp.where(r > 0, spill(jnp.maximum(r - 1, 0)), 0.0)
            out_ref[pl.ds(r * span, span), :] = (band(r) + above)[:span]
            return carry

        lax.fori_loop(0, geo.rows, one, 0)


def gather_own(geo, message, out_ref):
    devices = geo.rows * geo.cols
    if geo.own >= LANES:
        lines = geo.own // LANES
        for d in range(devices):
            out_ref[pl.ds(d * lines, lines), :] = message[d, Y_ROW : Y_ROW + lines, :]
    else:
        sharers = LANES // geo.own
        for t in range(devices // sharers):
            line = message[t * sharers, Y_ROW : Y_ROW + 1, :]
            for d in range(1, sharers):
                line = line + message[t * sharers + d, Y_ROW : Y_ROW + 1, :]
            out_ref[t : t + 1, :] = line


def product(geo, package_ref, sums_ref):
    groups = geo.own // SUBS
    totals = [jnp.zeros((SUBS, LANES), jnp.float32) for _ in range(groups)]
    for t in range(geo.lattice // LANES):
        line = jnp.broadcast_to(sums_ref[t : t + 1, :], (SUBS, LANES))
        for g in range(groups):
            block = package_ref[g * SUBS : (g + 1) * SUBS, t * LANES : (t + 1) * LANES]
            totals[g] = totals[g] + block * line
    return totals


def own_lines(geo, totals, start):
    per_line = min(len(totals), LANES // SUBS)
    sub = iota((SUBS, LANES), 0)
    lane = iota((SUBS, LANES), 1)
    lines = []
    for h in range(len(totals) // per_line):
        line = jnp.zeros((SUBS, LANES), jnp.float32)
        for q in range(per_line):
            column = jnp.sum(totals[h * per_line + q], axis=1, keepdims=True)
            line = jnp.where(lane == start + q * SUBS + sub, column, line)
        lines.append(jnp.sum(line, axis=0, keepdims=True))
    return lines


def own_start(geo, me):
    if geo.own >= LANES:
        return 0
    return (me % (LANES // geo.own)) * geo.own


def column_line(geo, field, at):
    sub = iota((SUBS, LANES), 0)
    lane = iota((SUBS, LANES), 1)
    total = jnp.zeros((SUBS, LANES), jnp.float32)
    for g in range(geo.height // SUBS):
        column = jnp.broadcast_to(field[g * SUBS : (g + 1) * SUBS, at : at + 1], (SUBS, LANES))
        total = total + jnp.where(lane == g * SUBS + sub, column, 0.0)
    return jnp.sum(total, axis=0, keepdims=True)


def line_column(geo, line):
    sub = iota((SUBS, LANES), 0)
    table = jnp.broadcast_to(line, (SUBS, LANES))
    return jnp.concatenate(
        [lookup(table, g * SUBS + sub) for g in range(geo.height // SUBS)], axis=0
    )


def beside(geo, field, east_line, west_line):
    lane = iota((geo.height, LANES), 1)
    extra = jnp.where(
        lane == 0,
        line_column(geo, east_line),
        jnp.where(lane == LANES - 1, line_column(geo, west_line), 0.0),
    )
    return jnp.concatenate([field, extra], axis=1)


def wide_lines(geo, line):
    return [line[:, q * LANES : (q + 1) * LANES] for q in range(geo.breadth // LANES)]


def wide_row(geo, message, sender, row=HALO_ROW):
    return jnp.concatenate(
        [message[sender, pl.ds(row + q, 1), :] for q in range(geo.breadth // LANES)], axis=1
    )


def tile_of(rows):
    empty = jnp.zeros((1, LANES), jnp.float32)
    return jnp.concatenate([rows.get(i, empty) for i in range(SUBS)], axis=0)


def put_all(ref, tile, offset=0):
    ref[:, offset : offset + SUBS, :] = jnp.broadcast_to(tile[None], (ref.shape[0],) + tile.shape)


def put(ref, target, row, lines):
    for i, line in enumerate(lines):
        ref[target, pl.ds(row + i, 1), :] = line


def share_rows(lines, spill):
    rows = {PIECE_ROW + i: line for i, line in enumerate(lines)}
    rows[SPILL_ROW] = spill
    return rows


def matrix(geo, state, top, low, top_wide, above, below):
    breadth = geo.breadth
    width = breadth + LANES
    after = pltpu.roll(top_wide, width - 1, 1)[:, :breadth]
    before = pltpu.roll(top_wide, 1, 1)[:, :breadth]
    row_at = iota((geo.height, breadth), 0)
    down = jnp.where(row_at == geo.height - 1, below, pltpu.roll(low, geo.height - 1, 0))
    up = jnp.where(row_at == 0, above, pltpu.roll(low, 1, 0))
    top_out = state(DIAG_T) * top - state(LINK_R) * after - state(LINK_L) * before - state(VIA) * low
    low_out = state(DIAG_B) * low - state(LINK_D) * down - state(LINK_U) * up - state(VIA) * top
    return top_out, low_out


def links(geo, row, col, wire_ref):
    height, breadth = geo.height, geo.breadth
    row_at = iota((height, breadth), 0)
    col_at = iota((height, breadth), 1)
    right = jnp.where((col == geo.cols - 1) & (col_at == breadth - 1), 0.0, wire_ref[0])
    down = jnp.where((row == geo.rows - 1) & (row_at == height - 1), 0.0, wire_ref[1])
    return right, down


def fetch(pairs, semaphores):
    copies = [
        pltpu.make_async_copy(source, target, semaphores.at[i])
        for i, (source, target) in enumerate(pairs)
    ]
    for copy in copies:
        copy.start()
    return copies


def open_kernel(geo, *refs):
    inputs, wave_ref, send, rel_ref = refs[:12], *refs[12:15]
    volt_ref, package_ref, decap_ref, decap_cond_ref, supply_ref, state_ref, source_ref = refs[15:22]
    map_ref, mask_ref, cond_ref, wire_ref, cap_ref, via_ref, load_ref, semaphores = refs[22:]
    early = (map_ref, mask_ref, cond_ref, volt_ref, wire_ref)
    late = (cap_ref, via_ref, load_ref, decap_ref, decap_cond_ref, supply_ref, package_ref)
    copies = fetch(tuple(zip(inputs, early + late)), semaphores)
    for copy in copies[: len(early)]:
        copy.wait()
    row, col = place()
    me, east, west, south, north = neighbours(geo, row, col)
    height, breadth = geo.height, geo.breadth
    own_level = row * geo.block_rows + iota((height, breadth), 0) // geo.tile_rows
    rel = lax.div(map_ref[...], jnp.int32(BC)) - own_level
    cond = spread(geo, cond_ref, row, col, rel, breadth // LANES)
    weight = mask_ref[...].astype(jnp.float32) * cond
    rel_ref[...] = rel
    top, low = volt_ref[0], volt_ref[1]
    right, down = links(geo, row, col, wire_ref)
    lines, spill = shares(geo, weight * top, rel, col)
    put_all(send, tile_of(share_rows(lines, spill)))
    put(send, east, HALO_ROW, [column_line(geo, top, breadth - 1), column_line(geo, right, breadth - 1)])
    put(send, west, HALO_ROW, [column_line(geo, top, 0)])
    put(send, north, HALO_ROW, wide_lines(geo, low[:1]))
    put(send, south, HALO_ROW, wide_lines(geo, low[height - 1 :]))
    put(send, south, Y_ROW, wide_lines(geo, down[height - 1 :]))
    for copy in copies[len(early) : -1]:
        copy.wait()
    via = via_ref[...]
    decap_cond = decap_cond_ref[...]
    frac = decap_cond / (1.0 + decap_cond)
    cap_top, cap_low = cap_ref[0], cap_ref[1]
    state_ref[LINK_R] = right
    state_ref[LINK_D] = down
    state_ref[VIA] = via
    state_ref[WEIGHT] = weight
    state_ref[DIAG_T] = cap_top + right + via + weight
    state_ref[DIAG_B] = cap_low + down + via + frac
    supply = spread(geo, supply_ref, row, col, rel, breadth // LANES)
    source_ref[0] = cap_top * top + weight * supply
    source_ref[1] = cap_low * low + frac * decap_ref[...] - wave_ref[0] * load_ref[...]
    copies[-1].wait()


def first_kernel(
    geo,
    message,
    package_ref,
    volt_ref,
    base_ref,
    source_ref,
    rel_ref,
    send,
    state_ref,
    residual_ref,
    direction_ref,
    sums_ref,
):
    row, col = place()
    me, east, west, south, north = neighbours(geo, row, col)
    height, breadth = geo.height, geo.breadth
    gather_shares(geo, message, 0, sums_ref)
    own = own_lines(geo, product(geo, package_ref, sums_ref), own_start(geo, me))

    rel = rel_ref[...]
    top, low = volt_ref[0], volt_ref[1]
    planes = {at: base_ref[at] for at in (LINK_R, LINK_D, VIA, WEIGHT)}
    weight, right, down = planes[WEIGHT], planes[LINK_R], planes[LINK_D]
    row_at = iota((height, breadth), 0)
    first_col = iota((height, LANES), 1) == 0
    edge = jnp.where(col > 0, message[west, HALO_ROW + 1 : HALO_ROW + 2, :], 0.0)
    left = pltpu.roll(right, 1, 1)
    left = jnp.concatenate(
        [jnp.where(first_col, line_column(geo, edge), left[:, :LANES]), left[:, LANES:]], axis=1
    )
    edge = jnp.where(row > 0, wide_row(geo, message, north, Y_ROW), 0.0)
    up = jnp.where(row_at == 0, edge, pltpu.roll(down, 1, 0))
    diag_top = base_ref[DIAG_T] + left
    diag_low = base_ref[DIAG_B] + up
    planes.update(
        {
            LINK_L: left,
            LINK_U: up,
            DIAG_T: diag_top,
            DIAG_B: diag_low,
            INV_T: 1.0 / diag_top,
            INV_B: 1.0 / diag_low,
        }
    )
    for at, plane in planes.items():
        state_ref[at] = plane
    wide = beside(
        geo,
        top,
        message[east, HALO_ROW : HALO_ROW + 1, :],
        message[west, HALO_ROW : HALO_ROW + 1, :],
    )
    top_out, low_out = matrix(
        geo,
        planes.__getitem__,
        top,
        low,
        wide,
        wide_row(geo, message, north),
        wide_row(geo, message, south),
    )
    residual_top = source_ref[0] - top_out
    residual_low = source_ref[1] - low_out
    residual_ref[0] = residual_top
    residual_ref[1] = residual_low
    gain = steps_of()[0][1]
    direction_top = gain * residual_top * planes[INV_T]
    direction_low = gain * residual_low * planes[INV_B]
    direction_ref[0] = direction_top
    direction_ref[1] = direction_low
    pull = weight * planes[INV_T]
    lines, spill = shares(geo, weight * direction_top, rel, col)
    rows = share_rows(lines, spill)
    rows.update({Y_ROW + i: line for i, line in enumerate(own)})
    put_all(send, tile_of(rows))
    lines, spill = shares(geo, weight * pull, rel, col)
    put_all(send, tile_of(share_rows(lines, spill)), SECOND)
    below = rel.astype(jnp.float32)
    for target, at in ((east, breadth - 1), (west, 0)):
        fields = (direction_top, pull, below)
        put(send, target, HALO_ROW, [column_line(geo, field, at) for field in fields])
    put(send, north, HALO_ROW, wide_lines(geo, direction_low[:1]))
    put(send, south, HALO_ROW, wide_lines(geo, direction_low[height - 1 :]))


def finish_direction(geo, message, product_ref, row, col, stage, direction, pull, rel):
    gain = steps_of()[stage][1]
    coupled = spread(geo, product_ref, row, col, rel, rel.shape[1] // LANES)
    return direction + gain * pull * coupled, coupled


def step_kernel(geo, stage, *refs):
    if stage == 1:
        (message, package_ref, state_ref, residual_in, direction_in, iterate_in, rel_ref) = refs[:7]
        (send, residual_ref, direction_ref, iterate_ref, pull_ref, wide_rel_ref, squares_ref) = refs[7:14]
    else:
        (message, package_ref, state_ref, residual_in, direction_in, iterate_in) = refs[:6]
        (pull_ref, wide_rel_ref, squares_ref) = refs[6:9]
        (send, iterate_ref) = refs[9:11]
        if stage < DEG - 1:
            (residual_ref, direction_ref) = refs[11:13]
    product_ref, sums_ref = refs[-2:]
    row, col = place()
    me, east, west, south, north = neighbours(geo, row, col)
    height, breadth = geo.height, geo.breadth
    gain_before = steps_of()[stage - 1][1]
    gather_own(geo, message, product_ref)
    gather_shares(geo, message, 0, sums_ref)
    if stage == 1:
        gather_shares(geo, message, SECOND, squares_ref)
    sums_ref[...] = sums_ref[...] + gain_before * squares_ref[...] * product_ref[...]
    own = own_lines(geo, product(geo, package_ref, sums_ref), own_start(geo, me))

    def state(at):
        return state_ref[at]

    weight = state(WEIGHT)
    if stage == 1:
        pull = beside(
            geo,
            weight * state(INV_T),
            message[east, HALO_ROW + 1 : HALO_ROW + 2, :],
            message[west, HALO_ROW + 1 : HALO_ROW + 2, :],
        )
        wide_rel = beside(
            geo,
            rel_ref[...].astype(jnp.float32),
            message[east, REL_ROW : REL_ROW + 1, :],
            message[west, REL_ROW : REL_ROW + 1, :],
        ).astype(jnp.int32)
        pull_ref[...] = pull
        wide_rel_ref[...] = wide_rel
    else:
        pull = pull_ref[...]
        wide_rel = wide_rel_ref[...]
    rel = wide_rel[:, :breadth]
    wide = beside(
        geo,
        direction_in[0],
        message[east, HALO_ROW : HALO_ROW + 1, :],
        message[west, HALO_ROW : HALO_ROW + 1, :],
    )
    wide, coupled = finish_direction(
        geo, message, product_ref, row, col, stage - 1, wide, pull, wide_rel
    )
    top = wide[:, :breadth]
    low = direction_in[1]
    top_out, low_out = matrix(
        geo,
        state,
        top,
        low,
        wide,
        wide_row(geo, message, north),
        wide_row(geo, message, south),
    )
    residual_top = residual_in[0] + weight * coupled[:, :breadth] - top_out
    residual_low = residual_in[1] - low_out
    keep, gain = steps_of()[stage]
    direction_top = keep * top + gain * residual_top * state(INV_T)
    direction_low = keep * low + gain * residual_low * state(INV_B)
    iterate_top = iterate_in[0] + top
    iterate_low = iterate_in[1] + low
    if stage == DEG - 1:
        iterate_top = iterate_top + direction_top
        iterate_low = iterate_low + direction_low
        lines, spill = shares(geo, weight * iterate_top, rel, col)
    else:
        residual_ref[0] = residual_top
        residual_ref[1] = residual_low
        direction_ref[0] = direction_top
        direction_ref[1] = direction_low
        lines, spill = shares(geo, weight * direction_top, rel, col)
    iterate_ref[0] = iterate_top
    iterate_ref[1] = iterate_low
    rows = share_rows(lines, spill)
    rows.update({Y_ROW + i: line for i, line in enumerate(own)})
    put_all(send, tile_of(rows))
    if stage < DEG - 1:
        put(send, east, HALO_ROW, [column_line(geo, direction_top, breadth - 1)])
        put(send, west, HALO_ROW, [column_line(geo, direction_top, 0)])
        put(send, north, HALO_ROW, wide_lines(geo, direction_low[:1]))
        put(send, south, HALO_ROW, wide_lines(geo, direction_low[height - 1 :]))


def last_kernel(
    geo,
    message,
    package_ref,
    iterate_ref,
    pull_ref,
    wide_rel_ref,
    squares_ref,
    decap_ref,
    decap_cond_ref,
    supply_ref,
    voltage_ref,
    decap_volt_ref,
    bump_volt_ref,
    product_ref,
    sums_ref,
):
    row, col = place()
    me = row * geo.cols + col
    breadth = geo.breadth
    gain = steps_of()[DEG - 1][1]
    gather_own(geo, message, product_ref)
    gather_shares(geo, message, 0, sums_ref)
    sums_ref[...] = sums_ref[...] + gain * squares_ref[...] * product_ref[...]
    own = own_lines(geo, product(geo, package_ref, sums_ref), 0)
    if geo.own >= LANES:
        supply = supply_ref[pl.ds(me * len(own), len(own)), :]
        bump_volt_ref[...] = supply + jnp.concatenate(own, axis=0)
    else:
        sharers = LANES // geo.own
        line = jnp.broadcast_to(supply_ref[pl.ds(me // sharers, 1), :], (SUBS, LANES))
        line = lookup(line, (iota((SUBS, LANES), 1) + own_start(geo, me)) % LANES)
        bump_volt_ref[...] = (line[:1] + own[0])[:, : geo.own]
    coupled = spread(
        geo, product_ref, row, col, wide_rel_ref[:, :breadth], breadth // LANES
    )
    low = iterate_ref[1]
    voltage_ref[0] = iterate_ref[0] + gain * pull_ref[:, :breadth] * coupled
    voltage_ref[1] = low
    decap_cond = decap_cond_ref[...]
    decap_volt_ref[...] = (decap_ref[...] + decap_cond * low) / (1.0 + decap_cond)


def exchange(message):
    return lax.all_to_all(message, AXES, split_axis=0, concat_axis=0, tiled=True)


def call(kernel, operands, outputs, scratch=(), outside=(), scalar=None):
    inside = pl.BlockSpec(memory_space=pltpu.VMEM)
    specs = [inside] * len(operands)
    if scalar is not None:
        specs[scalar] = pl.BlockSpec(memory_space=pltpu.SMEM)
    specs = [pl.BlockSpec(memory_space=pltpu.HBM)] * len(outside) + specs
    outside = [pltpu.with_memory_space_constraint(array, pltpu.HBM) for array in outside]
    out_specs = [
        pl.BlockSpec(memory_space=getattr(output, "memory_space", pltpu.VMEM)) for output in outputs
    ]
    return pl.pallas_call(
        kernel,
        out_shape=list(outputs),
        in_specs=specs,
        out_specs=out_specs,
        scratch_shapes=list(scratch),
        compiler_params=pltpu.CompilerParams(vmem_limit_bytes=16 * 2**20),
    )(*outside, *operands)


def shards(
    volt_start,
    cap_dt,
    wire_cond,
    via_cond,
    load_current,
    load_wave,
    decap_state,
    decap_cond,
    bump_map,
    via_mask,
    bump_cond,
    bump_supply,
    package,
):
    height, breadth = via_cond.shape
    rows, cols = lax.axis_size("row"), lax.axis_size("col")
    block_rows, block_cols = BR // rows, BC // cols
    own, lattice = package.shape
    geo = Geometry(
        height,
        breadth,
        rows,
        cols,
        own,
        block_rows,
        block_cols,
        height // block_rows,
        breadth // block_cols,
        lattice,
    )
    devices = rows * cols
    f32 = jnp.float32
    table = (lattice // LANES, LANES)
    cond = bump_cond.reshape(table)
    supply = bump_supply.reshape(table)
    field = pltpu.VMEM((height, breadth), f32)
    pair = pltpu.VMEM((2, height, breadth), f32)
    message = pltpu.VMEM((devices, SUBS, LANES), f32)
    held = pltpu.VMEM(table, f32)

    whole = pltpu.VMEM((height, breadth), jnp.int32)
    sent, rel, volt, package, decap, decap_cond, supply, base, source = call(
        functools.partial(open_kernel, geo),
        (load_wave,),
        (
            message,
            whole,
            pair,
            pltpu.VMEM(package.shape, f32),
            field,
            field,
            held,
            pltpu.VMEM((10, height, breadth), f32),
            pair,
        ),
        (whole, whole, held, pair, pair, field, field, pltpu.SemaphoreType.DMA((12,))),
        outside=(
            bump_map,
            via_mask,
            cond,
            volt_start,
            wire_cond,
            cap_dt,
            via_cond,
            load_current,
            decap_state,
            decap_cond,
            supply,
            package,
        ),
        scalar=0,
    )
    sent, state, residual, direction = call(
        functools.partial(first_kernel, geo),
        (exchange(sent), package, volt, base, source, rel),
        (
            pltpu.VMEM((devices, 2 * SUBS, LANES), f32),
            pltpu.VMEM((10, height, breadth), f32),
            pair,
            pair,
        ),
        (held,),
    )
    wide = (height, breadth + LANES)
    sent, residual, direction, iterate, pull, wide_rel, squares = call(
        functools.partial(step_kernel, geo, 1),
        (exchange(sent), package, state, residual, direction, volt, rel),
        (message, pair, pair, pair, pltpu.VMEM(wide, f32), pltpu.VMEM(wide, jnp.int32), held),
        (held, held),
    )
    for stage in range(2, DEG):
        sent, iterate, *carried = call(
            functools.partial(step_kernel, geo, stage),
            (
                exchange(sent),
                package,
                state,
                residual,
                direction,
                iterate,
                pull,
                wide_rel,
                squares,
            ),
            (message, pair, pair, pair) if stage < DEG - 1 else (message, pair),
            (held, held),
        )
        if carried:
            residual, direction = carried
    voltage, decap_volt, bump_volt = call(
        functools.partial(last_kernel, geo),
        (
            exchange(sent),
            package,
            iterate,
            pull,
            wide_rel,
            squares,
            decap,
            decap_cond,
            supply,
        ),
        (
            jax.ShapeDtypeStruct((2, height, breadth), f32),
            jax.ShapeDtypeStruct((height, breadth), f32),
            jax.ShapeDtypeStruct((max(1, own // LANES), min(own, LANES)), f32),
        ),
        (held, held),
    )
    return voltage, decap_volt, bump_volt.reshape(own)


def solution(mesh):
    field = P("row", "col")
    pair = P(None, "row", "col")
    return jax.shard_map(
        shards,
        mesh=mesh,
        in_specs=(
            pair,
            pair,
            pair,
            field,
            field,
            P(),
            field,
            field,
            field,
            field,
            P(),
            P(),
            P(AXES, None),
        ),
        out_specs=(pair, field, P(AXES)),
        check_vma=False,
    )
```

```python
import collections
import functools

import jax
import jax.numpy as jnp
from jax import lax
from jax.experimental import pallas as pl
from jax.experimental.pallas import tpu as pltpu
from jax.sharding import PartitionSpec as P

BR = 128
BC = 64
DEG = 4

CHEB_LO = 0.05
CHEB_HI = 2.0
CHEB_MID = (CHEB_HI + CHEB_LO) / 2.0
CHEB_HALF = (CHEB_HI - CHEB_LO) / 2.0
CHEB_RATIO = CHEB_MID / CHEB_HALF

LANES = 128
SUBS = 8
AXES = ("row", "col")

FIRST = ("share", "spill", "halo", "deep")
SECOND = ("own", "share", "spill", "square", "halo")
NEXT = ("own", "share", "spill", "halo")
LAST = ("own", "share", "spill")

(LINK_R, LINK_L, LINK_D, LINK_U, VIA, WEIGHT, DIAG_T, DIAG_B, INV_T, INV_B) = range(10)

Geometry = collections.namedtuple(
    "Geometry",
    [
        "height",
        "breadth",
        "rows",
        "cols",
        "own",
        "block_rows",
        "block_cols",
        "tile_rows",
        "tile_cols",
        "lattice",
    ],
)


def rows_of(geo, parts):
    sizes = {
        "own": max(1, geo.own // LANES),
        "share": -(-geo.block_rows * geo.block_cols // LANES),
        "square": -(-geo.block_rows * geo.block_cols // LANES),
        "spill": 1,
        "halo": geo.breadth // LANES,
        "deep": geo.breadth // LANES,
    }
    starts, end = {}, 0
    for part in parts:
        starts[part] = end
        end += sizes[part]
    starts["end"] = end
    return starts


def row_at(message, device, row):
    return message[device, :, row * LANES : (row + 1) * LANES]


def steps_of():
    factors = [(0.0, 1.0 / CHEB_MID)]
    rho_now = 1.0 / CHEB_RATIO
    for _ in range(DEG - 1):
        rho_next = 1.0 / (2.0 * CHEB_RATIO - rho_now)
        factors.append((rho_next * rho_now, 2.0 * rho_next / CHEB_HALF))
        rho_now = rho_next
    return factors


def iota(shape, dim):
    return lax.broadcasted_iota(jnp.int32, shape, dim)


def lookup(table, index):
    return jnp.take_along_axis(table, index, axis=1, mode="promise_in_bounds")


def place():
    row = lax.axis_index("row")
    col = lax.axis_index("col")
    return row, col


def neighbours(geo, row, col):
    me = row * geo.cols + col
    east = jnp.where(col < geo.cols - 1, me + 1, me)
    west = jnp.where(col > 0, me - 1, me)
    south = jnp.where(row < geo.rows - 1, me + geo.cols, me)
    north = jnp.where(row > 0, me - geo.cols, me)
    return me, east, west, south, north


def per_band(geo):
    return geo.block_rows * BC // LANES


def spread(geo, ref, row, col, rel, tiles):
    span = per_band(geo)
    base = row * span
    count = geo.lattice // LANES
    lines = [ref[pl.ds(base + t, 1), :] for t in range(span)]
    lines.append(ref[pl.ds(jnp.minimum(base + span, count - 1), 1), :])
    per_line = LANES // BC
    sub = iota((SUBS, LANES), 0)
    lane = iota((SUBS, LANES), 1)
    last = geo.breadth // LANES
    columns = []
    for q in range(tiles):
        if q < last:
            columns.append(col * geo.block_cols + (lane + q * LANES) // geo.tile_cols)
        else:
            after = jnp.minimum((col + 1) * geo.block_cols, BC - 1)
            before = jnp.maximum(col * geo.block_cols - 1, 0)
            columns.append(jnp.where(lane < LANES // 2, after, before))
    bands = []
    for g in range(geo.height // SUBS):
        picks = []
        for shift in (0, 1):
            levels = [(g * SUBS + i) // geo.tile_rows + shift for i in range(SUBS)]
            held = [level // per_line for level in levels]
            table = jnp.broadcast_to(lines[held[0]], (SUBS, LANES))
            for i in range(1, SUBS):
                if held[i] != held[i - 1]:
                    table = jnp.where(
                        sub >= i, jnp.broadcast_to(lines[held[i]], (SUBS, LANES)), table
                    )
            part = ((g * SUBS + sub) // geo.tile_rows + shift) % per_line
            picks.append([lookup(table, part * BC + columns[q]) for q in range(tiles)])
        bands.append(
            jnp.concatenate(
                [
                    jnp.where(
                        rel[g * SUBS : (g + 1) * SUBS, q * LANES : (q + 1) * LANES] == 0,
                        picks[0][q],
                        picks[1][q],
                    )
                    for q in range(tiles)
                ],
                axis=1,
            )
        )
    return jnp.concatenate(bands, axis=0)


def shares(geo, weighted, rel, col, half=0):
    height, breadth = geo.height, geo.breadth
    near = jnp.where(rel == 0, weighted, 0.0)
    both = jnp.concatenate([near, weighted - near], axis=0)
    high = both.astype(jnp.bfloat16)
    rest = both - high.astype(jnp.float32)
    mid = rest.astype(jnp.bfloat16)
    low = (rest - mid.astype(jnp.float32)).astype(jnp.bfloat16)
    adder = (
        iota((breadth, LANES), 0) // geo.tile_cols == iota((breadth, LANES), 1) % geo.block_cols
    )
    adder = adder.astype(jnp.float32).astype(jnp.bfloat16)
    summed = jnp.dot(
        jnp.concatenate([high, mid, low], axis=0), adder, preferred_element_type=jnp.float32
    )
    summed = summed[: 2 * height] + summed[2 * height : 4 * height] + summed[4 * height :]
    sub = iota((SUBS, LANES), 0)
    segment = iota((SUBS, LANES), 1) // geo.block_cols
    segments = LANES // geo.block_cols
    packed = -(-geo.block_rows // segments)
    slot = col + half * (BC // geo.block_cols)
    totals = [jnp.zeros((SUBS, LANES), jnp.float32) for _ in range(packed)]
    spill = jnp.zeros((SUBS, LANES), jnp.float32)
    for shift in (0, 1):
        for g in range(height // SUBS):
            first = g * SUBS // geo.tile_rows + shift
            final = (g * SUBS + SUBS - 1) // geo.tile_rows + shift
            level = (g * SUBS + sub) // geo.tile_rows + shift
            start = shift * height + g * SUBS
            block = summed[start : start + SUBS]
            for h in range(packed):
                if first < (h + 1) * segments and final >= h * segments:
                    hit = level == segment + h * segments
                    if final >= geo.block_rows:
                        hit = hit & (level < geo.block_rows)
                    totals[h] = totals[h] + jnp.where(hit, block, 0.0)
            if final >= geo.block_rows:
                hit = (level == geo.block_rows) & (segment == slot)
                spill = spill + jnp.where(hit, block, 0.0)
    lines = [jnp.sum(total, axis=0, keepdims=True) for total in totals]
    return lines, jnp.sum(spill, axis=0, keepdims=True)


def gather_shares(geo, message, starts, out_ref, part="share", half=0):
    span = per_band(geo)
    per_line = LANES // BC
    segments = LANES // geo.block_cols
    sub = iota((SUBS, LANES), 0)
    lane = iota((SUBS, LANES), 1)
    level = sub * per_line + lane // BC
    index = (level % segments) * geo.block_cols + lane % geo.block_cols
    owner = (lane % BC) // geo.block_cols
    packed = -(-geo.block_rows // segments)

    def band(r):
        total = jnp.zeros((SUBS, LANES), jnp.float32)
        for c in range(geo.cols):
            sender = r * geo.cols + c
            table = jnp.broadcast_to(row_at(message, sender, starts[part]), (SUBS, LANES))
            for h in range(1, packed):
                line = row_at(message, sender, starts[part] + h)
                table = jnp.where(
                    sub >= h * segments // per_line, jnp.broadcast_to(line, (SUBS, LANES)), table
                )
            total = jnp.where(owner == c, lookup(table, index), total)
        return total

    def spill(r):
        line = row_at(message, r * geo.cols, starts["spill"])
        for c in range(1, geo.cols):
            line = line + row_at(message, r * geo.cols + c, starts["spill"])
        line = jnp.broadcast_to(line, (SUBS, LANES))
        if half:
            line = pltpu.roll(line, LANES - half * BC, 1)
        return jnp.where((sub == 0) & (lane < BC), line, 0.0)

    if geo.rows <= 8:
        for r in range(geo.rows):
            total = band(r)
            if r > 0:
                total = total + spill(r - 1)
            out_ref[pl.ds(r * span, span), :] = total[:span]
    else:

        def one(r, carry):
            above = jnp.where(r > 0, spill(jnp.maximum(r - 1, 0)), 0.0)
            out_ref[pl.ds(r * span, span), :] = (band(r) + above)[:span]
            return carry

        lax.fori_loop(0, geo.rows, one, 0)


def gather_own(geo, message, starts, out_ref):
    devices = geo.rows * geo.cols
    if geo.own >= LANES:
        lines = geo.own // LANES
        for d in range(devices):
            for i in range(lines):
                at = d * lines + i
                out_ref[at : at + 1, :] = row_at(message, d, starts["own"] + i)
    else:
        sharers = LANES // geo.own
        for t in range(devices // sharers):
            line = row_at(message, t * sharers, starts["own"])
            for d in range(1, sharers):
                line = line + row_at(message, t * sharers + d, starts["own"])
            out_ref[t : t + 1, :] = line


def product(geo, package_ref, sums_ref):
    groups = geo.own // SUBS
    totals = [jnp.zeros((SUBS, LANES), jnp.float32) for _ in range(groups)]
    for t in range(geo.lattice // LANES):
        line = jnp.broadcast_to(sums_ref[t : t + 1, :], (SUBS, LANES))
        for g in range(groups):
            block = package_ref[g * SUBS : (g + 1) * SUBS, t * LANES : (t + 1) * LANES]
            totals[g] = totals[g] + block * line
    return totals


def own_lines(geo, totals, start):
    per_line = min(len(totals), LANES // SUBS)
    sub = iota((SUBS, LANES), 0)
    lane = iota((SUBS, LANES), 1)
    lines = []
    for h in range(len(totals) // per_line):
        line = jnp.zeros((SUBS, LANES), jnp.float32)
        for q in range(per_line):
            column = jnp.sum(totals[h * per_line + q], axis=1, keepdims=True)
            line = jnp.where(lane == start + q * SUBS + sub, column, line)
        lines.append(jnp.sum(line, axis=0, keepdims=True))
    return lines


def own_start(geo, me):
    if geo.own >= LANES:
        return 0
    return (me % (LANES // geo.own)) * geo.own


def column_line(geo, field, at, start=0):
    sub = iota((SUBS, LANES), 0)
    lane = iota((SUBS, LANES), 1)
    total = jnp.zeros((SUBS, LANES), jnp.float32)
    for g in range(geo.height // SUBS):
        column = jnp.broadcast_to(field[g * SUBS : (g + 1) * SUBS, at : at + 1], (SUBS, LANES))
        total = total + jnp.where(lane == start + g * SUBS + sub, column, 0.0)
    return jnp.sum(total, axis=0, keepdims=True)


def line_column(geo, line, start=0):
    sub = iota((SUBS, LANES), 0)
    table = jnp.broadcast_to(line, (SUBS, LANES))
    return jnp.concatenate(
        [lookup(table, start + g * SUBS + sub) for g in range(geo.height // SUBS)], axis=0
    )


def beside(geo, field, east_line, west_line, start=0):
    lane = iota((geo.height, LANES), 1)
    extra = jnp.where(
        lane == 0,
        line_column(geo, east_line, start),
        jnp.where(lane == LANES - 1, line_column(geo, west_line, start), 0.0),
    )
    return jnp.concatenate([field, extra], axis=1)


def wide_lines(geo, line):
    return [line[:, q * LANES : (q + 1) * LANES] for q in range(geo.breadth // LANES)]


def wide_row(geo, message, sender, row):
    return jnp.concatenate(
        [row_at(message, sender, row + q) for q in range(geo.breadth // LANES)], axis=1
    )


def put_all(ref, row, lines):
    for i, line in enumerate(lines):
        to = (row + i) * LANES
        ref[:, :, to : to + LANES] = jnp.broadcast_to(line[None], (ref.shape[0], 1, LANES))


def put(ref, target, row, lines):
    for i, line in enumerate(lines):
        to = (row + i) * LANES
        ref[target, :, to : to + LANES] = line


def blank(geo):
    return [jnp.zeros((1, LANES), jnp.float32)] * (geo.breadth // LANES)


def matrix(geo, state, top, low, top_wide, above, below):
    breadth = geo.breadth
    width = breadth + LANES
    after = pltpu.roll(top_wide, width - 1, 1)[:, :breadth]
    before = pltpu.roll(top_wide, 1, 1)[:, :breadth]
    line_at = iota((geo.height, breadth), 0)
    down = jnp.where(line_at == geo.height - 1, below, pltpu.roll(low, geo.height - 1, 0))
    up = jnp.where(line_at == 0, above, pltpu.roll(low, 1, 0))
    top_out = state(DIAG_T) * top - state(LINK_R) * after - state(LINK_L) * before - state(VIA) * low
    low_out = state(DIAG_B) * low - state(LINK_D) * down - state(LINK_U) * up - state(VIA) * top
    return top_out, low_out


def links(geo, row, col, wire_ref):
    height, breadth = geo.height, geo.breadth
    line_at = iota((height, breadth), 0)
    col_at = iota((height, breadth), 1)
    right = jnp.where((col == geo.cols - 1) & (col_at == breadth - 1), 0.0, wire_ref[0])
    down = jnp.where((row == geo.rows - 1) & (line_at == height - 1), 0.0, wire_ref[1])
    return right, down


def fetch(pairs, semaphores):
    copies = [
        pltpu.make_async_copy(source, target, semaphores.at[i])
        for i, (source, target) in enumerate(pairs)
    ]
    for copy in copies:
        copy.start()
    return copies


def open_kernel(geo, *refs):
    inputs, wave_ref, send, rel_ref = refs[:12], *refs[12:15]
    volt_ref, package_ref, decap_ref, decap_cond_ref, supply_ref, state_ref, source_ref = refs[15:22]
    map_ref, mask_ref, cond_ref, wire_ref, cap_ref, via_ref, load_ref, semaphores = refs[22:]
    early = (map_ref, mask_ref, cond_ref, volt_ref, wire_ref)
    late = (cap_ref, via_ref, load_ref, decap_ref, decap_cond_ref, supply_ref, package_ref)
    copies = fetch(tuple(zip(inputs, early + late)), semaphores)
    for copy in copies[: len(early)]:
        copy.wait()
    row, col = place()
    me, east, west, south, north = neighbours(geo, row, col)
    height, breadth = geo.height, geo.breadth
    own_level = row * geo.block_rows + iota((height, breadth), 0) // geo.tile_rows
    rel = lax.div(map_ref[...], jnp.int32(BC)) - own_level
    cond = spread(geo, cond_ref, row, col, rel, breadth // LANES)
    weight = mask_ref[...].astype(jnp.float32) * cond
    rel_ref[...] = rel
    top, low = volt_ref[0], volt_ref[1]
    right, down = links(geo, row, col, wire_ref)
    lines, spill = shares(geo, weight * top, rel, col)
    starts = rows_of(geo, FIRST)
    halo = starts["halo"]
    put_all(send, starts["share"], lines + [spill])
    put(send, me, halo, blank(geo))
    put(send, east, halo, [column_line(geo, top, breadth - 1), column_line(geo, right, breadth - 1)])
    put(send, west, halo, [column_line(geo, top, 0)])
    put(send, north, halo, wide_lines(geo, low[:1]))
    put(send, south, halo, wide_lines(geo, low[height - 1 :]))
    put(send, south, starts["deep"], wide_lines(geo, down[height - 1 :]))
    for copy in copies[len(early) : -1]:
        copy.wait()
    via = via_ref[...]
    decap_cond = decap_cond_ref[...]
    frac = decap_cond / (1.0 + decap_cond)
    cap_top, cap_low = cap_ref[0], cap_ref[1]
    state_ref[LINK_R] = right
    state_ref[LINK_D] = down
    state_ref[VIA] = via
    state_ref[WEIGHT] = weight
    state_ref[DIAG_T] = cap_top + right + via + weight
    state_ref[DIAG_B] = cap_low + down + via + frac
    supply = spread(geo, supply_ref, row, col, rel, breadth // LANES)
    source_ref[0] = cap_top * top + weight * supply
    source_ref[1] = cap_low * low + frac * decap_ref[...] - wave_ref[0] * load_ref[...]
    copies[-1].wait()


def first_kernel(
    geo,
    message,
    package_ref,
    volt_ref,
    base_ref,
    source_ref,
    rel_ref,
    send,
    state_ref,
    residual_ref,
    direction_ref,
    sums_ref,
):
    row, col = place()
    me, east, west, south, north = neighbours(geo, row, col)
    height, breadth = geo.height, geo.breadth
    starts = rows_of(geo, FIRST)
    halo = starts["halo"]
    gather_shares(geo, message, starts, sums_ref)
    own = own_lines(geo, product(geo, package_ref, sums_ref), own_start(geo, me))

    rel = rel_ref[...]
    top, low = volt_ref[0], volt_ref[1]
    planes = {at: base_ref[at] for at in (LINK_R, LINK_D, VIA, WEIGHT)}
    weight, right, down = planes[WEIGHT], planes[LINK_R], planes[LINK_D]
    line_at = iota((height, breadth), 0)
    first_col = iota((height, LANES), 1) == 0
    edge = jnp.where(col > 0, row_at(message, west, halo + 1), 0.0)
    left = pltpu.roll(right, 1, 1)
    left = jnp.concatenate(
        [jnp.where(first_col, line_column(geo, edge), left[:, :LANES]), left[:, LANES:]], axis=1
    )
    edge = jnp.where(row > 0, wide_row(geo, message, north, starts["deep"]), 0.0)
    up = jnp.where(line_at == 0, edge, pltpu.roll(down, 1, 0))
    diag_top = base_ref[DIAG_T] + left
    diag_low = base_ref[DIAG_B] + up
    planes.update(
        {
            LINK_L: left,
            LINK_U: up,
            DIAG_T: diag_top,
            DIAG_B: diag_low,
            INV_T: 1.0 / diag_top,
            INV_B: 1.0 / diag_low,
        }
    )
    for at, plane in planes.items():
        state_ref[at] = plane
    wide = beside(
        geo,
        top,
        row_at(message, east, halo),
        row_at(message, west, halo),
    )
    top_out, low_out = matrix(
        geo,
        planes.__getitem__,
        top,
        low,
        wide,
        wide_row(geo, message, north, halo),
        wide_row(geo, message, south, halo),
    )
    residual_top = source_ref[0] - top_out
    residual_low = source_ref[1] - low_out
    residual_ref[0] = residual_top
    residual_ref[1] = residual_low
    gain = steps_of()[0][1]
    direction_top = gain * residual_top * planes[INV_T]
    direction_low = gain * residual_low * planes[INV_B]
    direction_ref[0] = direction_top
    direction_ref[1] = direction_low
    pull = weight * planes[INV_T]
    lines, spill = shares(geo, weight * direction_top, rel, col)
    square_lines, square_spill = shares(geo, weight * pull, rel, col, 1)
    starts = rows_of(geo, SECOND)
    halo = starts["halo"]
    put_all(send, starts["own"], own + lines + [spill + square_spill] + square_lines)
    put(send, me, halo, blank(geo))
    below = rel.astype(jnp.float32)
    for target, at in ((east, breadth - 1), (west, 0)):
        both = column_line(geo, pull, at) + column_line(geo, below, at, LANES // 2)
        put(send, target, halo, [column_line(geo, direction_top, at), both])
    put(send, north, halo, wide_lines(geo, direction_low[:1]))
    put(send, south, halo, wide_lines(geo, direction_low[height - 1 :]))


def finish_direction(geo, message, product_ref, row, col, stage, direction, pull, rel):
    gain = steps_of()[stage][1]
    coupled = spread(geo, product_ref, row, col, rel, rel.shape[1] // LANES)
    return direction + gain * pull * coupled, coupled


def step_kernel(geo, stage, *refs):
    if stage == 1:
        (message, package_ref, state_ref, residual_in, direction_in, iterate_in, rel_ref) = refs[:7]
        (send, residual_ref, direction_ref, iterate_ref, pull_ref, wide_rel_ref, squares_ref) = refs[7:14]
    else:
        (message, package_ref, state_ref, residual_in, direction_in, iterate_in) = refs[:6]
        (pull_ref, wide_rel_ref, squares_ref) = refs[6:9]
        (send, iterate_ref) = refs[9:11]
        if stage < DEG - 1:
            (residual_ref, direction_ref) = refs[11:13]
    product_ref, sums_ref = refs[-2:]
    row, col = place()
    me, east, west, south, north = neighbours(geo, row, col)
    height, breadth = geo.height, geo.breadth
    gain_before = steps_of()[stage - 1][1]
    starts = rows_of(geo, SECOND if stage == 1 else NEXT)
    halo = starts["halo"]
    gather_own(geo, message, starts, product_ref)
    gather_shares(geo, message, starts, sums_ref)
    if stage == 1:
        gather_shares(geo, message, starts, squares_ref, "square", 1)
    sums_ref[...] = sums_ref[...] + gain_before * squares_ref[...] * product_ref[...]
    own = own_lines(geo, product(geo, package_ref, sums_ref), own_start(geo, me))

    def state(at):
        return state_ref[at]

    weight = state(WEIGHT)
    if stage == 1:
        pull = beside(
            geo,
            weight * state(INV_T),
            row_at(message, east, halo + 1),
            row_at(message, west, halo + 1),
        )
        wide_rel = beside(
            geo,
            rel_ref[...].astype(jnp.float32),
            row_at(message, east, halo + 1),
            row_at(message, west, halo + 1),
            LANES // 2,
        ).astype(jnp.int32)
        pull_ref[...] = pull
        wide_rel_ref[...] = wide_rel
    else:
        pull = pull_ref[...]
        wide_rel = wide_rel_ref[...]
    rel = wide_rel[:, :breadth]
    wide = beside(
        geo,
        direction_in[0],
        row_at(message, east, halo),
        row_at(message, west, halo),
    )
    wide, coupled = finish_direction(
        geo, message, product_ref, row, col, stage - 1, wide, pull, wide_rel
    )
    top = wide[:, :breadth]
    low = direction_in[1]
    top_out, low_out = matrix(
        geo,
        state,
        top,
        low,
        wide,
        wide_row(geo, message, north, halo),
        wide_row(geo, message, south, halo),
    )
    residual_top = residual_in[0] + weight * coupled[:, :breadth] - top_out
    residual_low = residual_in[1] - low_out
    keep, gain = steps_of()[stage]
    direction_top = keep * top + gain * residual_top * state(INV_T)
    direction_low = keep * low + gain * residual_low * state(INV_B)
    iterate_top = iterate_in[0] + top
    iterate_low = iterate_in[1] + low
    if stage == DEG - 1:
        iterate_top = iterate_top + direction_top
        iterate_low = iterate_low + direction_low
        lines, spill = shares(geo, weight * iterate_top, rel, col)
    else:
        residual_ref[0] = residual_top
        residual_ref[1] = residual_low
        direction_ref[0] = direction_top
        direction_ref[1] = direction_low
        lines, spill = shares(geo, weight * direction_top, rel, col)
    iterate_ref[0] = iterate_top
    iterate_ref[1] = iterate_low
    starts = rows_of(geo, NEXT if stage < DEG - 1 else LAST)
    put_all(send, starts["own"], own + lines + [spill])
    if stage < DEG - 1:
        halo = starts["halo"]
        put(send, me, halo, blank(geo))
        put(send, east, halo, [column_line(geo, direction_top, breadth - 1)])
        put(send, west, halo, [column_line(geo, direction_top, 0)])
        put(send, north, halo, wide_lines(geo, direction_low[:1]))
        put(send, south, halo, wide_lines(geo, direction_low[height - 1 :]))


def last_kernel(
    geo,
    message,
    package_ref,
    iterate_ref,
    pull_ref,
    wide_rel_ref,
    squares_ref,
    decap_ref,
    decap_cond_ref,
    supply_ref,
    voltage_ref,
    decap_volt_ref,
    bump_volt_ref,
    product_ref,
    sums_ref,
):
    row, col = place()
    me = row * geo.cols + col
    breadth = geo.breadth
    gain = steps_of()[DEG - 1][1]
    starts = rows_of(geo, LAST)
    gather_own(geo, message, starts, product_ref)
    gather_shares(geo, message, starts, sums_ref)
    sums_ref[...] = sums_ref[...] + gain * squares_ref[...] * product_ref[...]
    own = own_lines(geo, product(geo, package_ref, sums_ref), 0)
    if geo.own >= LANES:
        supply = supply_ref[pl.ds(me * len(own), len(own)), :]
        bump_volt_ref[...] = supply + jnp.concatenate(own, axis=0)
    else:
        sharers = LANES // geo.own
        line = jnp.broadcast_to(supply_ref[pl.ds(me // sharers, 1), :], (SUBS, LANES))
        line = lookup(line, (iota((SUBS, LANES), 1) + own_start(geo, me)) % LANES)
        bump_volt_ref[...] = (line[:1] + own[0])[:, : geo.own]
    coupled = spread(
        geo, product_ref, row, col, wide_rel_ref[:, :breadth], breadth // LANES
    )
    low = iterate_ref[1]
    voltage_ref[0] = iterate_ref[0] + gain * pull_ref[:, :breadth] * coupled
    voltage_ref[1] = low
    decap_cond = decap_cond_ref[...]
    decap_volt_ref[...] = (decap_ref[...] + decap_cond * low) / (1.0 + decap_cond)


def exchange(message):
    return lax.all_to_all(message, AXES, split_axis=0, concat_axis=0, tiled=True)


def call(kernel, operands, outputs, scratch=(), outside=(), scalar=None):
    inside = pl.BlockSpec(memory_space=pltpu.VMEM)
    specs = [inside] * len(operands)
    if scalar is not None:
        specs[scalar] = pl.BlockSpec(memory_space=pltpu.SMEM)
    specs = [pl.BlockSpec(memory_space=pltpu.HBM)] * len(outside) + specs
    outside = [pltpu.with_memory_space_constraint(array, pltpu.HBM) for array in outside]
    out_specs = [
        pl.BlockSpec(memory_space=getattr(output, "memory_space", pltpu.VMEM)) for output in outputs
    ]
    return pl.pallas_call(
        kernel,
        out_shape=list(outputs),
        in_specs=specs,
        out_specs=out_specs,
        scratch_shapes=list(scratch),
        compiler_params=pltpu.CompilerParams(vmem_limit_bytes=16 * 2**20),
    )(*outside, *operands)


def shards(
    volt_start,
    cap_dt,
    wire_cond,
    via_cond,
    load_current,
    load_wave,
    decap_state,
    decap_cond,
    bump_map,
    via_mask,
    bump_cond,
    bump_supply,
    package,
):
    height, breadth = via_cond.shape
    rows, cols = lax.axis_size("row"), lax.axis_size("col")
    block_rows, block_cols = BR // rows, BC // cols
    own, lattice = package.shape
    geo = Geometry(
        height,
        breadth,
        rows,
        cols,
        own,
        block_rows,
        block_cols,
        height // block_rows,
        breadth // block_cols,
        lattice,
    )
    devices = rows * cols
    f32 = jnp.float32
    table = (lattice // LANES, LANES)
    cond = bump_cond.reshape(table)
    supply = bump_supply.reshape(table)
    field = pltpu.VMEM((height, breadth), f32)
    pair = pltpu.VMEM((2, height, breadth), f32)

    def message(parts):
        return pltpu.VMEM((devices, 1, rows_of(geo, parts)["end"] * LANES), f32)

    held = pltpu.VMEM(table, f32)

    whole = pltpu.VMEM((height, breadth), jnp.int32)
    sent, rel, volt, package, decap, decap_cond, supply, base, source = call(
        functools.partial(open_kernel, geo),
        (load_wave,),
        (
            message(FIRST),
            whole,
            pair,
            pltpu.VMEM(package.shape, f32),
            field,
            field,
            held,
            pltpu.VMEM((10, height, breadth), f32),
            pair,
        ),
        (whole, whole, held, pair, pair, field, field, pltpu.SemaphoreType.DMA((12,))),
        outside=(
            bump_map,
            via_mask,
            cond,
            volt_start,
            wire_cond,
            cap_dt,
            via_cond,
            load_current,
            decap_state,
            decap_cond,
            supply,
            package,
        ),
        scalar=0,
    )
    sent, state, residual, direction = call(
        functools.partial(first_kernel, geo),
        (exchange(sent), package, volt, base, source, rel),
        (
            message(SECOND),
            pltpu.VMEM((10, height, breadth), f32),
            pair,
            pair,
        ),
        (held,),
    )
    wide = (height, breadth + LANES)
    sent, residual, direction, iterate, pull, wide_rel, squares = call(
        functools.partial(step_kernel, geo, 1),
        (exchange(sent), package, state, residual, direction, volt, rel),
        (message(NEXT), pair, pair, pair, pltpu.VMEM(wide, f32), pltpu.VMEM(wide, jnp.int32), held),
        (held, held),
    )
    for stage in range(2, DEG):
        sent, iterate, *carried = call(
            functools.partial(step_kernel, geo, stage),
            (
                exchange(sent),
                package,
                state,
                residual,
                direction,
                iterate,
                pull,
                wide_rel,
                squares,
            ),
            (message(NEXT), pair, pair, pair) if stage < DEG - 1 else (message(LAST), pair),
            (held, held),
        )
        if carried:
            residual, direction = carried
    voltage, decap_volt, bump_volt = call(
        functools.partial(last_kernel, geo),
        (
            exchange(sent),
            package,
            iterate,
            pull,
            wide_rel,
            squares,
            decap,
            decap_cond,
            supply,
        ),
        (
            jax.ShapeDtypeStruct((2, height, breadth), f32),
            jax.ShapeDtypeStruct((height, breadth), f32),
            jax.ShapeDtypeStruct((max(1, own // LANES), min(own, LANES)), f32),
        ),
        (held, held),
    )
    return voltage, decap_volt, bump_volt.reshape(own)


def solution(mesh):
    field = P("row", "col")
    pair = P(None, "row", "col")
    return jax.shard_map(
        shards,
        mesh=mesh,
        in_specs=(
            pair,
            pair,
            pair,
            field,
            field,
            P(),
            field,
            field,
            field,
            field,
            P(),
            P(),
            P(AXES, None),
        ),
        out_specs=(pair, field, P(AXES)),
        check_vma=False,
    )
```

```python
import collections
import functools

import jax
import jax.numpy as jnp
from jax import lax
from jax.experimental import pallas as pl
from jax.experimental.pallas import tpu as pltpu
from jax.sharding import PartitionSpec as P

BR = 128
BC = 64
DEG = 4

CHEB_LO = 0.05
CHEB_HI = 2.0
CHEB_MID = (CHEB_HI + CHEB_LO) / 2.0
CHEB_HALF = (CHEB_HI - CHEB_LO) / 2.0
CHEB_RATIO = CHEB_MID / CHEB_HALF

LANES = 128
SUBS = 8
AXES = ("row", "col")

FIRST = ("share", "spill", "halo", "deep")
SECOND = ("own", "share", "spill", "square", "halo")
NEXT = ("own", "share", "spill", "halo")
LAST = ("own", "share", "spill")

OPENING = 5

(LINK_R, LINK_L, LINK_D, LINK_U, VIA, WEIGHT, DIAG_T, DIAG_B, INV_T, INV_B) = range(10)

Geometry = collections.namedtuple(
    "Geometry",
    [
        "height",
        "breadth",
        "rows",
        "cols",
        "own",
        "block_rows",
        "block_cols",
        "tile_rows",
        "tile_cols",
        "lattice",
    ],
)


def rows_of(geo, parts):
    sizes = {
        "own": max(1, geo.own // LANES),
        "share": -(-geo.block_rows * geo.block_cols // LANES),
        "square": -(-geo.block_rows * geo.block_cols // LANES),
        "spill": 1,
        "halo": geo.breadth // LANES,
        "deep": geo.breadth // LANES,
    }
    starts, end = {}, 0
    for part in parts:
        starts[part] = end
        end += sizes[part]
    starts["end"] = end
    return starts


def row_at(message, device, row):
    return message[device, :, row * LANES : (row + 1) * LANES]


def steps_of():
    factors = [(0.0, 1.0 / CHEB_MID)]
    rho_now = 1.0 / CHEB_RATIO
    for _ in range(DEG - 1):
        rho_next = 1.0 / (2.0 * CHEB_RATIO - rho_now)
        factors.append((rho_next * rho_now, 2.0 * rho_next / CHEB_HALF))
        rho_now = rho_next
    return factors


def iota(shape, dim):
    return lax.broadcasted_iota(jnp.int32, shape, dim)


def lookup(table, index):
    return jnp.take_along_axis(table, index, axis=1, mode="promise_in_bounds")


def place():
    row = lax.axis_index("row")
    col = lax.axis_index("col")
    return row, col


def neighbours(geo, row, col):
    me = row * geo.cols + col
    east = jnp.where(col < geo.cols - 1, me + 1, me)
    west = jnp.where(col > 0, me - 1, me)
    south = jnp.where(row < geo.rows - 1, me + geo.cols, me)
    north = jnp.where(row > 0, me - geo.cols, me)
    return me, east, west, south, north


def per_band(geo):
    return geo.block_rows * BC // LANES


def spread(geo, ref, row, col, rel, tiles):
    span = per_band(geo)
    base = row * span
    count = geo.lattice // LANES
    lines = [ref[pl.ds(base + t, 1), :] for t in range(span)]
    lines.append(ref[pl.ds(jnp.minimum(base + span, count - 1), 1), :])
    per_line = LANES // BC
    sub = iota((SUBS, LANES), 0)
    lane = iota((SUBS, LANES), 1)
    last = geo.breadth // LANES
    columns = []
    for q in range(tiles):
        if q < last:
            columns.append(col * geo.block_cols + (lane + q * LANES) // geo.tile_cols)
        else:
            after = jnp.minimum((col + 1) * geo.block_cols, BC - 1)
            before = jnp.maximum(col * geo.block_cols - 1, 0)
            columns.append(jnp.where(lane < LANES // 2, after, before))
    bands = []
    for g in range(geo.height // SUBS):
        picks = []
        for shift in (0, 1):
            levels = [(g * SUBS + i) // geo.tile_rows + shift for i in range(SUBS)]
            held = [level // per_line for level in levels]
            table = jnp.broadcast_to(lines[held[0]], (SUBS, LANES))
            for i in range(1, SUBS):
                if held[i] != held[i - 1]:
                    table = jnp.where(
                        sub >= i, jnp.broadcast_to(lines[held[i]], (SUBS, LANES)), table
                    )
            part = ((g * SUBS + sub) // geo.tile_rows + shift) % per_line
            picks.append([lookup(table, part * BC + columns[q]) for q in range(tiles)])
        bands.append(
            jnp.concatenate(
                [
                    jnp.where(
                        rel[g * SUBS : (g + 1) * SUBS, q * LANES : (q + 1) * LANES] == 0,
                        picks[0][q],
                        picks[1][q],
                    )
                    for q in range(tiles)
                ],
                axis=1,
            )
        )
    return jnp.concatenate(bands, axis=0)


def shares(geo, weighted, rel, col, half=0):
    height, breadth = geo.height, geo.breadth
    near = jnp.where(rel == 0, weighted, 0.0)
    both = jnp.concatenate([near, weighted - near], axis=0)
    high = both.astype(jnp.bfloat16)
    rest = both - high.astype(jnp.float32)
    mid = rest.astype(jnp.bfloat16)
    low = (rest - mid.astype(jnp.float32)).astype(jnp.bfloat16)
    adder = (
        iota((breadth, LANES), 0) // geo.tile_cols == iota((breadth, LANES), 1) % geo.block_cols
    )
    adder = adder.astype(jnp.float32).astype(jnp.bfloat16)
    summed = jnp.dot(
        jnp.concatenate([high, mid, low], axis=0), adder, preferred_element_type=jnp.float32
    )
    summed = summed[: 2 * height] + summed[2 * height : 4 * height] + summed[4 * height :]
    sub = iota((SUBS, LANES), 0)
    segment = iota((SUBS, LANES), 1) // geo.block_cols
    segments = LANES // geo.block_cols
    packed = -(-geo.block_rows // segments)
    slot = col + half * (BC // geo.block_cols)
    totals = [jnp.zeros((SUBS, LANES), jnp.float32) for _ in range(packed)]
    spill = jnp.zeros((SUBS, LANES), jnp.float32)
    for shift in (0, 1):
        for g in range(height // SUBS):
            first = g * SUBS // geo.tile_rows + shift
            final = (g * SUBS + SUBS - 1) // geo.tile_rows + shift
            level = (g * SUBS + sub) // geo.tile_rows + shift
            start = shift * height + g * SUBS
            block = summed[start : start + SUBS]
            for h in range(packed):
                if first < (h + 1) * segments and final >= h * segments:
                    hit = level == segment + h * segments
                    if final >= geo.block_rows:
                        hit = hit & (level < geo.block_rows)
                    totals[h] = totals[h] + jnp.where(hit, block, 0.0)
            if final >= geo.block_rows:
                hit = (level == geo.block_rows) & (segment == slot)
                spill = spill + jnp.where(hit, block, 0.0)
    lines = [jnp.sum(total, axis=0, keepdims=True) for total in totals]
    return lines, jnp.sum(spill, axis=0, keepdims=True)


def gather_shares(geo, message, starts, out_ref, part="share", half=0):
    span = per_band(geo)
    per_line = LANES // BC
    segments = LANES // geo.block_cols
    sub = iota((SUBS, LANES), 0)
    lane = iota((SUBS, LANES), 1)
    level = sub * per_line + lane // BC
    index = (level % segments) * geo.block_cols + lane % geo.block_cols
    owner = (lane % BC) // geo.block_cols
    packed = -(-geo.block_rows // segments)

    def band(r):
        total = jnp.zeros((SUBS, LANES), jnp.float32)
        for c in range(geo.cols):
            sender = r * geo.cols + c
            table = jnp.broadcast_to(row_at(message, sender, starts[part]), (SUBS, LANES))
            for h in range(1, packed):
                line = row_at(message, sender, starts[part] + h)
                table = jnp.where(
                    sub >= h * segments // per_line, jnp.broadcast_to(line, (SUBS, LANES)), table
                )
            total = jnp.where(owner == c, lookup(table, index), total)
        return total

    def spill(r):
        line = row_at(message, r * geo.cols, starts["spill"])
        for c in range(1, geo.cols):
            line = line + row_at(message, r * geo.cols + c, starts["spill"])
        line = jnp.broadcast_to(line, (SUBS, LANES))
        if half:
            line = pltpu.roll(line, LANES - half * BC, 1)
        return jnp.where((sub == 0) & (lane < BC), line, 0.0)

    if geo.rows <= 8:
        for r in range(geo.rows):
            total = band(r)
            if r > 0:
                total = total + spill(r - 1)
            out_ref[pl.ds(r * span, span), :] = total[:span]
    else:

        def one(r, carry):
            above = jnp.where(r > 0, spill(jnp.maximum(r - 1, 0)), 0.0)
            out_ref[pl.ds(r * span, span), :] = (band(r) + above)[:span]
            return carry

        lax.fori_loop(0, geo.rows, one, 0)


def gather_own(geo, message, starts, out_ref):
    devices = geo.rows * geo.cols
    if geo.own >= LANES:
        lines = geo.own // LANES
        for d in range(devices):
            for i in range(lines):
                at = d * lines + i
                out_ref[at : at + 1, :] = row_at(message, d, starts["own"] + i)
    else:
        sharers = LANES // geo.own
        for t in range(devices // sharers):
            line = row_at(message, t * sharers, starts["own"])
            for d in range(1, sharers):
                line = line + row_at(message, t * sharers + d, starts["own"])
            out_ref[t : t + 1, :] = line


def product(geo, package_ref, sums_ref):
    groups = package_ref.shape[0] // SUBS
    totals = [jnp.zeros((SUBS, LANES), jnp.float32) for _ in range(groups)]
    for t in range(geo.lattice // LANES):
        line = jnp.broadcast_to(sums_ref[t : t + 1, :], (SUBS, LANES))
        for g in range(groups):
            block = package_ref[g * SUBS : (g + 1) * SUBS, t * LANES : (t + 1) * LANES]
            totals[g] = totals[g] + block * line
    return totals


def products(geo, package_refs, sums_ref):
    return [total for ref in package_refs for total in product(geo, ref, sums_ref)]


def own_lines(geo, totals, start):
    per_line = min(len(totals), LANES // SUBS)
    sub = iota((SUBS, LANES), 0)
    lane = iota((SUBS, LANES), 1)
    lines = []
    for h in range(len(totals) // per_line):
        line = jnp.zeros((SUBS, LANES), jnp.float32)
        for q in range(per_line):
            column = jnp.sum(totals[h * per_line + q], axis=1, keepdims=True)
            line = jnp.where(lane == start + q * SUBS + sub, column, line)
        lines.append(jnp.sum(line, axis=0, keepdims=True))
    return lines


def own_start(geo, me):
    if geo.own >= LANES:
        return 0
    return (me % (LANES // geo.own)) * geo.own


def column_line(geo, field, at, start=0):
    sub = iota((SUBS, LANES), 0)
    lane = iota((SUBS, LANES), 1)
    total = jnp.zeros((SUBS, LANES), jnp.float32)
    for g in range(geo.height // SUBS):
        column = jnp.broadcast_to(field[g * SUBS : (g + 1) * SUBS, at : at + 1], (SUBS, LANES))
        total = total + jnp.where(lane == start + g * SUBS + sub, column, 0.0)
    return jnp.sum(total, axis=0, keepdims=True)


def line_column(geo, line, start=0):
    sub = iota((SUBS, LANES), 0)
    table = jnp.broadcast_to(line, (SUBS, LANES))
    return jnp.concatenate(
        [lookup(table, start + g * SUBS + sub) for g in range(geo.height // SUBS)], axis=0
    )


def beside(geo, field, east_line, west_line, start=0):
    lane = iota((geo.height, LANES), 1)
    extra = jnp.where(
        lane == 0,
        line_column(geo, east_line, start),
        jnp.where(lane == LANES - 1, line_column(geo, west_line, start), 0.0),
    )
    return jnp.concatenate([field, extra], axis=1)


def wide_lines(geo, line):
    return [line[:, q * LANES : (q + 1) * LANES] for q in range(geo.breadth // LANES)]


def wide_row(geo, message, sender, row):
    return jnp.concatenate(
        [row_at(message, sender, row + q) for q in range(geo.breadth // LANES)], axis=1
    )


def put_all(ref, row, lines):
    for i, line in enumerate(lines):
        to = (row + i) * LANES
        ref[:, :, to : to + LANES] = jnp.broadcast_to(line[None], (ref.shape[0], 1, LANES))


def put(ref, target, row, lines):
    for i, line in enumerate(lines):
        to = (row + i) * LANES
        ref[target, :, to : to + LANES] = line


def blank(geo):
    return [jnp.zeros((1, LANES), jnp.float32)] * (geo.breadth // LANES)


def matrix(geo, state, top, low, top_wide, above, below):
    breadth = geo.breadth
    width = breadth + LANES
    after = pltpu.roll(top_wide, width - 1, 1)[:, :breadth]
    before = pltpu.roll(top_wide, 1, 1)[:, :breadth]
    line_at = iota((geo.height, breadth), 0)
    down = jnp.where(line_at == geo.height - 1, below, pltpu.roll(low, geo.height - 1, 0))
    up = jnp.where(line_at == 0, above, pltpu.roll(low, 1, 0))
    top_out = state(DIAG_T) * top - state(LINK_R) * after - state(LINK_L) * before - state(VIA) * low
    low_out = state(DIAG_B) * low - state(LINK_D) * down - state(LINK_U) * up - state(VIA) * top
    return top_out, low_out


def links(geo, row, col, wire_ref):
    height, breadth = geo.height, geo.breadth
    line_at = iota((height, breadth), 0)
    col_at = iota((height, breadth), 1)
    right = jnp.where((col == geo.cols - 1) & (col_at == breadth - 1), 0.0, wire_ref[0])
    down = jnp.where((row == geo.rows - 1) & (line_at == height - 1), 0.0, wire_ref[1])
    return right, down


def fetch(pairs, semaphores):
    copies = [
        pltpu.make_async_copy(source, target, semaphores.at[i])
        for i, (source, target) in enumerate(pairs)
    ]
    for copy in copies:
        copy.start()
    return copies


def open_kernel(geo, *refs):
    inputs, wave_ref, send, rel_ref = refs[:12], *refs[12:15]
    volt_ref, package_ref, decap_ref, decap_cond_ref, supply_ref, state_ref, source_ref = refs[15:22]
    map_ref, mask_ref, cond_ref, wire_ref, cap_ref, via_ref, load_ref, semaphores = refs[22:]
    early = (map_ref, mask_ref, cond_ref, volt_ref, wire_ref)
    late = (cap_ref, via_ref, load_ref, decap_ref, decap_cond_ref, supply_ref, package_ref)
    inputs = inputs[:-1] + (inputs[-1].at[: package_ref.shape[0], :],)
    copies = fetch(tuple(zip(inputs, early + late)), semaphores)
    for copy in copies[: len(early)]:
        copy.wait()
    row, col = place()
    me, east, west, south, north = neighbours(geo, row, col)
    height, breadth = geo.height, geo.breadth
    own_level = row * geo.block_rows + iota((height, breadth), 0) // geo.tile_rows
    rel = lax.div(map_ref[...], jnp.int32(BC)) - own_level
    cond = spread(geo, cond_ref, row, col, rel, breadth // LANES)
    weight = mask_ref[...].astype(jnp.float32) * cond
    rel_ref[...] = rel
    top, low = volt_ref[0], volt_ref[1]
    right, down = links(geo, row, col, wire_ref)
    lines, spill = shares(geo, weight * top, rel, col)
    starts = rows_of(geo, FIRST)
    halo = starts["halo"]
    put_all(send, starts["share"], lines + [spill])
    put(send, me, halo, blank(geo))
    put(send, east, halo, [column_line(geo, top, breadth - 1), column_line(geo, right, breadth - 1)])
    put(send, west, halo, [column_line(geo, top, 0)])
    put(send, north, halo, wide_lines(geo, low[:1]))
    put(send, south, halo, wide_lines(geo, low[height - 1 :]))
    put(send, south, starts["deep"], wide_lines(geo, down[height - 1 :]))
    for copy in copies[len(early) : -1]:
        copy.wait()
    via = via_ref[...]
    decap_cond = decap_cond_ref[...]
    frac = decap_cond / (1.0 + decap_cond)
    cap_top, cap_low = cap_ref[0], cap_ref[1]
    state_ref[LINK_R] = right
    state_ref[LINK_D] = down
    state_ref[VIA] = via
    state_ref[WEIGHT] = weight
    state_ref[DIAG_T] = cap_top + right + via + weight
    state_ref[DIAG_B] = cap_low + down + via + frac
    supply = spread(geo, supply_ref, row, col, rel, breadth // LANES)
    source_ref[0] = cap_top * top + weight * supply
    source_ref[1] = cap_low * low + frac * decap_ref[...] - wave_ref[0] * load_ref[...]
    copies[-1].wait()


def first_kernel(
    geo,
    package_in,
    message,
    package_ref,
    volt_ref,
    base_ref,
    source_ref,
    rel_ref,
    send,
    state_ref,
    residual_ref,
    direction_ref,
    package_more_ref,
    sums_ref,
    semaphore,
):
    rows_here = package_ref.shape[0]
    more = pltpu.make_async_copy(
        package_in.at[rows_here : geo.own, :], package_more_ref, semaphore
    )
    more.start()
    row, col = place()
    me, east, west, south, north = neighbours(geo, row, col)
    height, breadth = geo.height, geo.breadth
    starts = rows_of(geo, FIRST)
    halo = starts["halo"]
    gather_shares(geo, message, starts, sums_ref)
    totals = product(geo, package_ref, sums_ref)

    rel = rel_ref[...]
    top, low = volt_ref[0], volt_ref[1]
    planes = {at: base_ref[at] for at in (LINK_R, LINK_D, VIA, WEIGHT)}
    weight, right, down = planes[WEIGHT], planes[LINK_R], planes[LINK_D]
    line_at = iota((height, breadth), 0)
    first_col = iota((height, LANES), 1) == 0
    edge = jnp.where(col > 0, row_at(message, west, halo + 1), 0.0)
    left = pltpu.roll(right, 1, 1)
    left = jnp.concatenate(
        [jnp.where(first_col, line_column(geo, edge), left[:, :LANES]), left[:, LANES:]], axis=1
    )
    edge = jnp.where(row > 0, wide_row(geo, message, north, starts["deep"]), 0.0)
    up = jnp.where(line_at == 0, edge, pltpu.roll(down, 1, 0))
    diag_top = base_ref[DIAG_T] + left
    diag_low = base_ref[DIAG_B] + up
    planes.update(
        {
            LINK_L: left,
            LINK_U: up,
            DIAG_T: diag_top,
            DIAG_B: diag_low,
            INV_T: 1.0 / diag_top,
            INV_B: 1.0 / diag_low,
        }
    )
    for at, plane in planes.items():
        state_ref[at] = plane
    wide = beside(
        geo,
        top,
        row_at(message, east, halo),
        row_at(message, west, halo),
    )
    top_out, low_out = matrix(
        geo,
        planes.__getitem__,
        top,
        low,
        wide,
        wide_row(geo, message, north, halo),
        wide_row(geo, message, south, halo),
    )
    residual_top = source_ref[0] - top_out
    residual_low = source_ref[1] - low_out
    residual_ref[0] = residual_top
    residual_ref[1] = residual_low
    gain = steps_of()[0][1]
    direction_top = gain * residual_top * planes[INV_T]
    direction_low = gain * residual_low * planes[INV_B]
    direction_ref[0] = direction_top
    direction_ref[1] = direction_low
    pull = weight * planes[INV_T]
    lines, spill = shares(geo, weight * direction_top, rel, col)
    square_lines, square_spill = shares(geo, weight * pull, rel, col, 1)
    starts = rows_of(geo, SECOND)
    halo = starts["halo"]
    put_all(send, starts["share"], lines + [spill + square_spill] + square_lines)
    put(send, me, halo, blank(geo))
    below = rel.astype(jnp.float32)
    for target, at in ((east, breadth - 1), (west, 0)):
        both = column_line(geo, pull, at) + column_line(geo, below, at, LANES // 2)
        put(send, target, halo, [column_line(geo, direction_top, at), both])
    put(send, north, halo, wide_lines(geo, direction_low[:1]))
    put(send, south, halo, wide_lines(geo, direction_low[height - 1 :]))
    more.wait()
    totals = totals + product(geo, package_more_ref, sums_ref)
    put_all(send, starts["own"], own_lines(geo, totals, own_start(geo, me)))


def finish_direction(geo, message, product_ref, row, col, stage, direction, pull, rel):
    gain = steps_of()[stage][1]
    coupled = spread(geo, product_ref, row, col, rel, rel.shape[1] // LANES)
    return direction + gain * pull * coupled, coupled


def step_kernel(geo, stage, *refs):
    package_refs, refs = refs[:2], refs[2:]
    if stage == 1:
        (message, state_ref, residual_in, direction_in, iterate_in, rel_ref) = refs[:6]
        (send, residual_ref, direction_ref, iterate_ref, pull_ref, wide_rel_ref, squares_ref) = refs[6:13]
    else:
        (message, state_ref, residual_in, direction_in, iterate_in) = refs[:5]
        (pull_ref, wide_rel_ref, squares_ref) = refs[5:8]
        (send, iterate_ref) = refs[8:10]
        if stage < DEG - 1:
            (residual_ref, direction_ref) = refs[10:12]
    product_ref, sums_ref = refs[-2:]
    row, col = place()
    me, east, west, south, north = neighbours(geo, row, col)
    height, breadth = geo.height, geo.breadth
    gain_before = steps_of()[stage - 1][1]
    starts = rows_of(geo, SECOND if stage == 1 else NEXT)
    halo = starts["halo"]
    gather_own(geo, message, starts, product_ref)
    gather_shares(geo, message, starts, sums_ref)
    if stage == 1:
        gather_shares(geo, message, starts, squares_ref, "square", 1)
    sums_ref[...] = sums_ref[...] + gain_before * squares_ref[...] * product_ref[...]
    own = own_lines(geo, products(geo, package_refs, sums_ref), own_start(geo, me))

    def state(at):
        return state_ref[at]

    weight = state(WEIGHT)
    if stage == 1:
        pull = beside(
            geo,
            weight * state(INV_T),
            row_at(message, east, halo + 1),
            row_at(message, west, halo + 1),
        )
        wide_rel = beside(
            geo,
            rel_ref[...].astype(jnp.float32),
            row_at(message, east, halo + 1),
            row_at(message, west, halo + 1),
            LANES // 2,
        ).astype(jnp.int32)
        pull_ref[...] = pull
        wide_rel_ref[...] = wide_rel
    else:
        pull = pull_ref[...]
        wide_rel = wide_rel_ref[...]
    rel = wide_rel[:, :breadth]
    wide = beside(
        geo,
        direction_in[0],
        row_at(message, east, halo),
        row_at(message, west, halo),
    )
    wide, coupled = finish_direction(
        geo, message, product_ref, row, col, stage - 1, wide, pull, wide_rel
    )
    top = wide[:, :breadth]
    low = direction_in[1]
    top_out, low_out = matrix(
        geo,
        state,
        top,
        low,
        wide,
        wide_row(geo, message, north, halo),
        wide_row(geo, message, south, halo),
    )
    residual_top = residual_in[0] + weight * coupled[:, :breadth] - top_out
    residual_low = residual_in[1] - low_out
    keep, gain = steps_of()[stage]
    direction_top = keep * top + gain * residual_top * state(INV_T)
    direction_low = keep * low + gain * residual_low * state(INV_B)
    iterate_top = iterate_in[0] + top
    iterate_low = iterate_in[1] + low
    if stage == DEG - 1:
        iterate_top = iterate_top + direction_top
        iterate_low = iterate_low + direction_low
        lines, spill = shares(geo, weight * iterate_top, rel, col)
    else:
        residual_ref[0] = residual_top
        residual_ref[1] = residual_low
        direction_ref[0] = direction_top
        direction_ref[1] = direction_low
        lines, spill = shares(geo, weight * direction_top, rel, col)
    iterate_ref[0] = iterate_top
    iterate_ref[1] = iterate_low
    starts = rows_of(geo, NEXT if stage < DEG - 1 else LAST)
    put_all(send, starts["own"], own + lines + [spill])
    if stage < DEG - 1:
        halo = starts["halo"]
        put(send, me, halo, blank(geo))
        put(send, east, halo, [column_line(geo, direction_top, breadth - 1)])
        put(send, west, halo, [column_line(geo, direction_top, 0)])
        put(send, north, halo, wide_lines(geo, direction_low[:1]))
        put(send, south, halo, wide_lines(geo, direction_low[height - 1 :]))


def last_kernel(
    geo,
    package_ref,
    package_more_ref,
    message,
    iterate_ref,
    pull_ref,
    wide_rel_ref,
    squares_ref,
    decap_ref,
    decap_cond_ref,
    supply_ref,
    voltage_ref,
    decap_volt_ref,
    bump_volt_ref,
    product_ref,
    sums_ref,
):
    row, col = place()
    me = row * geo.cols + col
    breadth = geo.breadth
    gain = steps_of()[DEG - 1][1]
    starts = rows_of(geo, LAST)
    gather_own(geo, message, starts, product_ref)
    gather_shares(geo, message, starts, sums_ref)
    sums_ref[...] = sums_ref[...] + gain * squares_ref[...] * product_ref[...]
    own = own_lines(geo, products(geo, (package_ref, package_more_ref), sums_ref), 0)
    if geo.own >= LANES:
        supply = supply_ref[pl.ds(me * len(own), len(own)), :]
        bump_volt_ref[...] = supply + jnp.concatenate(own, axis=0)
    else:
        sharers = LANES // geo.own
        line = jnp.broadcast_to(supply_ref[pl.ds(me // sharers, 1), :], (SUBS, LANES))
        line = lookup(line, (iota((SUBS, LANES), 1) + own_start(geo, me)) % LANES)
        bump_volt_ref[...] = (line[:1] + own[0])[:, : geo.own]
    coupled = spread(
        geo, product_ref, row, col, wide_rel_ref[:, :breadth], breadth // LANES
    )
    low = iterate_ref[1]
    voltage_ref[0] = iterate_ref[0] + gain * pull_ref[:, :breadth] * coupled
    voltage_ref[1] = low
    decap_cond = decap_cond_ref[...]
    decap_volt_ref[...] = (decap_ref[...] + decap_cond * low) / (1.0 + decap_cond)


def exchange(message):
    return lax.all_to_all(message, AXES, split_axis=0, concat_axis=0, tiled=True)


def call(kernel, operands, outputs, scratch=(), outside=(), scalar=None):
    inside = pl.BlockSpec(memory_space=pltpu.VMEM)
    specs = [inside] * len(operands)
    if scalar is not None:
        specs[scalar] = pl.BlockSpec(memory_space=pltpu.SMEM)
    specs = [pl.BlockSpec(memory_space=pltpu.HBM)] * len(outside) + specs
    outside = [pltpu.with_memory_space_constraint(array, pltpu.HBM) for array in outside]
    out_specs = [
        pl.BlockSpec(memory_space=getattr(output, "memory_space", pltpu.VMEM)) for output in outputs
    ]
    return pl.pallas_call(
        kernel,
        out_shape=list(outputs),
        in_specs=specs,
        out_specs=out_specs,
        scratch_shapes=list(scratch),
        compiler_params=pltpu.CompilerParams(vmem_limit_bytes=16 * 2**20),
    )(*outside, *operands)


def shards(
    volt_start,
    cap_dt,
    wire_cond,
    via_cond,
    load_current,
    load_wave,
    decap_state,
    decap_cond,
    bump_map,
    via_mask,
    bump_cond,
    bump_supply,
    package,
):
    height, breadth = via_cond.shape
    rows, cols = lax.axis_size("row"), lax.axis_size("col")
    block_rows, block_cols = BR // rows, BC // cols
    own, lattice = package.shape
    geo = Geometry(
        height,
        breadth,
        rows,
        cols,
        own,
        block_rows,
        block_cols,
        height // block_rows,
        breadth // block_cols,
        lattice,
    )
    devices = rows * cols
    here = own * OPENING // SUBS // SUBS * SUBS
    f32 = jnp.float32
    table = (lattice // LANES, LANES)
    cond = bump_cond.reshape(table)
    supply = bump_supply.reshape(table)
    field = pltpu.VMEM((height, breadth), f32)
    pair = pltpu.VMEM((2, height, breadth), f32)

    def message(parts):
        return pltpu.VMEM((devices, 1, rows_of(geo, parts)["end"] * LANES), f32)

    held = pltpu.VMEM(table, f32)

    whole = pltpu.VMEM((height, breadth), jnp.int32)
    sent, rel, volt, package_here, decap, decap_cond, supply, base, source = call(
        functools.partial(open_kernel, geo),
        (load_wave,),
        (
            message(FIRST),
            whole,
            pair,
            pltpu.VMEM((here, lattice), f32),
            field,
            field,
            held,
            pltpu.VMEM((10, height, breadth), f32),
            pair,
        ),
        (whole, whole, held, pair, pair, field, field, pltpu.SemaphoreType.DMA((12,))),
        outside=(
            bump_map,
            via_mask,
            cond,
            volt_start,
            wire_cond,
            cap_dt,
            via_cond,
            load_current,
            decap_state,
            decap_cond,
            supply,
            package,
        ),
        scalar=0,
    )
    sent, state, residual, direction, package_more = call(
        functools.partial(first_kernel, geo),
        (exchange(sent), package_here, volt, base, source, rel),
        (
            message(SECOND),
            pltpu.VMEM((10, height, breadth), f32),
            pair,
            pair,
            pltpu.VMEM((own - here, lattice), f32),
        ),
        (held, pltpu.SemaphoreType.DMA),
        outside=(package,),
    )
    wide = (height, breadth + LANES)
    sent, residual, direction, iterate, pull, wide_rel, squares = call(
        functools.partial(step_kernel, geo, 1),
        (package_here, package_more, exchange(sent), state, residual, direction, volt, rel),
        (message(NEXT), pair, pair, pair, pltpu.VMEM(wide, f32), pltpu.VMEM(wide, jnp.int32), held),
        (held, held),
    )
    for stage in range(2, DEG):
        sent, iterate, *carried = call(
            functools.partial(step_kernel, geo, stage),
            (
                package_here,
                package_more,
                exchange(sent),
                state,
                residual,
                direction,
                iterate,
                pull,
                wide_rel,
                squares,
            ),
            (message(NEXT), pair, pair, pair) if stage < DEG - 1 else (message(LAST), pair),
            (held, held),
        )
        if carried:
            residual, direction = carried
    voltage, decap_volt, bump_volt = call(
        functools.partial(last_kernel, geo),
        (
            package_here,
            package_more,
            exchange(sent),
            iterate,
            pull,
            wide_rel,
            squares,
            decap,
            decap_cond,
            supply,
        ),
        (
            jax.ShapeDtypeStruct((2, height, breadth), f32),
            jax.ShapeDtypeStruct((height, breadth), f32),
            jax.ShapeDtypeStruct((max(1, own // LANES), min(own, LANES)), f32),
        ),
        (held, held),
    )
    return voltage, decap_volt, bump_volt.reshape(own)


def solution(mesh):
    field = P("row", "col")
    pair = P(None, "row", "col")
    return jax.shard_map(
        shards,
        mesh=mesh,
        in_specs=(
            pair,
            pair,
            pair,
            field,
            field,
            P(),
            field,
            field,
            field,
            field,
            P(),
            P(),
            P(AXES, None),
        ),
        out_specs=(pair, field, P(AXES)),
        check_vma=False,
    )
```

```python
import collections
import functools

import jax
import jax.numpy as jnp
from jax import lax
from jax.experimental import pallas as pl
from jax.experimental.pallas import tpu as pltpu
from jax.sharding import PartitionSpec as P

BR = 128
BC = 64
DEG = 4

CHEB_LO = 0.05
CHEB_HI = 2.0
CHEB_MID = (CHEB_HI + CHEB_LO) / 2.0
CHEB_HALF = (CHEB_HI - CHEB_LO) / 2.0
CHEB_RATIO = CHEB_MID / CHEB_HALF

LANES = 128
SUBS = 8
AXES = ("row", "col")

FIRST = ("share", "spill", "halo", "deep")
SECOND = ("own", "share", "spill", "square", "halo")
NEXT = ("own", "share", "spill", "halo")
LAST = ("own", "share", "spill")

OPENING = 7

(LINK_R, LINK_L, LINK_D, LINK_U, VIA, WEIGHT, DIAG_T, DIAG_B, INV_T, INV_B) = range(10)

Geometry = collections.namedtuple(
    "Geometry",
    [
        "height",
        "breadth",
        "rows",
        "cols",
        "own",
        "block_rows",
        "block_cols",
        "tile_rows",
        "tile_cols",
        "lattice",
    ],
)


def rows_of(geo, parts):
    sizes = {
        "own": max(1, geo.own // LANES),
        "share": -(-geo.block_rows * geo.block_cols // LANES),
        "square": -(-geo.block_rows * geo.block_cols // LANES),
        "spill": 1,
        "halo": geo.breadth // LANES,
        "deep": geo.breadth // LANES,
    }
    starts, end = {}, 0
    for part in parts:
        starts[part] = end
        end += sizes[part]
    starts["end"] = end
    return starts


def row_at(message, device, row):
    return message[device, :, row * LANES : (row + 1) * LANES]


def steps_of():
    factors = [(0.0, 1.0 / CHEB_MID)]
    rho_now = 1.0 / CHEB_RATIO
    for _ in range(DEG - 1):
        rho_next = 1.0 / (2.0 * CHEB_RATIO - rho_now)
        factors.append((rho_next * rho_now, 2.0 * rho_next / CHEB_HALF))
        rho_now = rho_next
    return factors


def iota(shape, dim):
    return lax.broadcasted_iota(jnp.int32, shape, dim)


def lookup(table, index):
    return jnp.take_along_axis(table, index, axis=1, mode="promise_in_bounds")


def place():
    row = lax.axis_index("row")
    col = lax.axis_index("col")
    return row, col


def neighbours(geo, row, col):
    me = row * geo.cols + col
    east = jnp.where(col < geo.cols - 1, me + 1, me)
    west = jnp.where(col > 0, me - 1, me)
    south = jnp.where(row < geo.rows - 1, me + geo.cols, me)
    north = jnp.where(row > 0, me - geo.cols, me)
    return me, east, west, south, north


def per_band(geo):
    return geo.block_rows * BC // LANES


def spread(geo, ref, row, col, rel, tiles):
    span = per_band(geo)
    base = row * span
    count = geo.lattice // LANES
    lines = [ref[pl.ds(base + t, 1), :] for t in range(span)]
    lines.append(ref[pl.ds(jnp.minimum(base + span, count - 1), 1), :])
    per_line = LANES // BC
    sub = iota((SUBS, LANES), 0)
    lane = iota((SUBS, LANES), 1)
    last = geo.breadth // LANES
    columns = []
    for q in range(tiles):
        if q < last:
            columns.append(col * geo.block_cols + (lane + q * LANES) // geo.tile_cols)
        else:
            after = jnp.minimum((col + 1) * geo.block_cols, BC - 1)
            before = jnp.maximum(col * geo.block_cols - 1, 0)
            columns.append(jnp.where(lane < LANES // 2, after, before))
    bands = []
    for g in range(geo.height // SUBS):
        picks = []
        for shift in (0, 1):
            levels = [(g * SUBS + i) // geo.tile_rows + shift for i in range(SUBS)]
            held = [level // per_line for level in levels]
            table = jnp.broadcast_to(lines[held[0]], (SUBS, LANES))
            for i in range(1, SUBS):
                if held[i] != held[i - 1]:
                    table = jnp.where(
                        sub >= i, jnp.broadcast_to(lines[held[i]], (SUBS, LANES)), table
                    )
            part = ((g * SUBS + sub) // geo.tile_rows + shift) % per_line
            picks.append([lookup(table, part * BC + columns[q]) for q in range(tiles)])
        bands.append(
            jnp.concatenate(
                [
                    jnp.where(
                        rel[g * SUBS : (g + 1) * SUBS, q * LANES : (q + 1) * LANES] == 0,
                        picks[0][q],
                        picks[1][q],
                    )
                    for q in range(tiles)
                ],
                axis=1,
            )
        )
    return jnp.concatenate(bands, axis=0)


def shares(geo, weighted, rel, col, half=0):
    height, breadth = geo.height, geo.breadth
    near = jnp.where(rel == 0, weighted, 0.0)
    both = jnp.concatenate([near, weighted - near], axis=0)
    high = both.astype(jnp.bfloat16)
    rest = both - high.astype(jnp.float32)
    mid = rest.astype(jnp.bfloat16)
    low = (rest - mid.astype(jnp.float32)).astype(jnp.bfloat16)
    adder = (
        iota((breadth, LANES), 0) // geo.tile_cols == iota((breadth, LANES), 1) % geo.block_cols
    )
    adder = adder.astype(jnp.float32).astype(jnp.bfloat16)
    summed = jnp.dot(
        jnp.concatenate([high, mid, low], axis=0), adder, preferred_element_type=jnp.float32
    )
    summed = summed[: 2 * height] + summed[2 * height : 4 * height] + summed[4 * height :]
    sub = iota((SUBS, LANES), 0)
    segment = iota((SUBS, LANES), 1) // geo.block_cols
    segments = LANES // geo.block_cols
    packed = -(-geo.block_rows // segments)
    slot = col + half * (BC // geo.block_cols)
    totals = [jnp.zeros((SUBS, LANES), jnp.float32) for _ in range(packed)]
    spill = jnp.zeros((SUBS, LANES), jnp.float32)
    for shift in (0, 1):
        for g in range(height // SUBS):
            first = g * SUBS // geo.tile_rows + shift
            final = (g * SUBS + SUBS - 1) // geo.tile_rows + shift
            level = (g * SUBS + sub) // geo.tile_rows + shift
            start = shift * height + g * SUBS
            block = summed[start : start + SUBS]
            for h in range(packed):
                if first < (h + 1) * segments and final >= h * segments:
                    hit = level == segment + h * segments
                    if final >= geo.block_rows:
                        hit = hit & (level < geo.block_rows)
                    totals[h] = totals[h] + jnp.where(hit, block, 0.0)
            if final >= geo.block_rows:
                hit = (level == geo.block_rows) & (segment == slot)
                spill = spill + jnp.where(hit, block, 0.0)
    lines = [jnp.sum(total, axis=0, keepdims=True) for total in totals]
    return lines, jnp.sum(spill, axis=0, keepdims=True)


def gather_shares(geo, message, starts, out_ref, part="share", half=0):
    span = per_band(geo)
    per_line = LANES // BC
    segments = LANES // geo.block_cols
    sub = iota((SUBS, LANES), 0)
    lane = iota((SUBS, LANES), 1)
    level = sub * per_line + lane // BC
    index = (level % segments) * geo.block_cols + lane % geo.block_cols
    owner = (lane % BC) // geo.block_cols
    packed = -(-geo.block_rows // segments)

    def band(r):
        total = jnp.zeros((SUBS, LANES), jnp.float32)
        for c in range(geo.cols):
            sender = r * geo.cols + c
            table = jnp.broadcast_to(row_at(message, sender, starts[part]), (SUBS, LANES))
            for h in range(1, packed):
                line = row_at(message, sender, starts[part] + h)
                table = jnp.where(
                    sub >= h * segments // per_line, jnp.broadcast_to(line, (SUBS, LANES)), table
                )
            total = jnp.where(owner == c, lookup(table, index), total)
        return total

    def spill(r):
        line = row_at(message, r * geo.cols, starts["spill"])
        for c in range(1, geo.cols):
            line = line + row_at(message, r * geo.cols + c, starts["spill"])
        line = jnp.broadcast_to(line, (SUBS, LANES))
        if half:
            line = pltpu.roll(line, LANES - half * BC, 1)
        return jnp.where((sub == 0) & (lane < BC), line, 0.0)

    if geo.rows <= 8:
        for r in range(geo.rows):
            total = band(r)
            if r > 0:
                total = total + spill(r - 1)
            out_ref[pl.ds(r * span, span), :] = total[:span]
    else:

        def one(r, carry):
            above = jnp.where(r > 0, spill(jnp.maximum(r - 1, 0)), 0.0)
            out_ref[pl.ds(r * span, span), :] = (band(r) + above)[:span]
            return carry

        lax.fori_loop(0, geo.rows, one, 0)


def gather_own(geo, message, starts, out_ref):
    devices = geo.rows * geo.cols
    if geo.own >= LANES:
        lines = geo.own // LANES
        for d in range(devices):
            for i in range(lines):
                at = d * lines + i
                out_ref[at : at + 1, :] = row_at(message, d, starts["own"] + i)
    else:
        sharers = LANES // geo.own
        for t in range(devices // sharers):
            line = row_at(message, t * sharers, starts["own"])
            for d in range(1, sharers):
                line = line + row_at(message, t * sharers + d, starts["own"])
            out_ref[t : t + 1, :] = line


def product(geo, package_ref, sums_ref):
    groups = package_ref.shape[0] // SUBS
    totals = [jnp.zeros((SUBS, LANES), jnp.float32) for _ in range(groups)]
    for t in range(geo.lattice // LANES):
        line = jnp.broadcast_to(sums_ref[t : t + 1, :], (SUBS, LANES))
        for g in range(groups):
            block = package_ref[g * SUBS : (g + 1) * SUBS, t * LANES : (t + 1) * LANES]
            totals[g] = totals[g] + block * line
    return totals


def products(geo, package_refs, sums_ref):
    return [total for ref in package_refs for total in product(geo, ref, sums_ref)]


def own_lines(geo, totals, start):
    per_line = min(len(totals), LANES // SUBS)
    sub = iota((SUBS, LANES), 0)
    lane = iota((SUBS, LANES), 1)
    lines = []
    for h in range(len(totals) // per_line):
        line = jnp.zeros((SUBS, LANES), jnp.float32)
        for q in range(per_line):
            column = jnp.sum(totals[h * per_line + q], axis=1, keepdims=True)
            line = jnp.where(lane == start + q * SUBS + sub, column, line)
        lines.append(jnp.sum(line, axis=0, keepdims=True))
    return lines


def own_start(geo, me):
    if geo.own >= LANES:
        return 0
    return (me % (LANES // geo.own)) * geo.own


def column_line(geo, field, at, start=0):
    sub = iota((SUBS, LANES), 0)
    lane = iota((SUBS, LANES), 1)
    total = jnp.zeros((SUBS, LANES), jnp.float32)
    for g in range(geo.height // SUBS):
        column = jnp.broadcast_to(field[g * SUBS : (g + 1) * SUBS, at : at + 1], (SUBS, LANES))
        total = total + jnp.where(lane == start + g * SUBS + sub, column, 0.0)
    return jnp.sum(total, axis=0, keepdims=True)


def line_column(geo, line, start=0):
    sub = iota((SUBS, LANES), 0)
    table = jnp.broadcast_to(line, (SUBS, LANES))
    return jnp.concatenate(
        [lookup(table, start + g * SUBS + sub) for g in range(geo.height // SUBS)], axis=0
    )


def beside(geo, field, east_line, west_line, start=0):
    lane = iota((geo.height, LANES), 1)
    extra = jnp.where(
        lane == 0,
        line_column(geo, east_line, start),
        jnp.where(lane == LANES - 1, line_column(geo, west_line, start), 0.0),
    )
    return jnp.concatenate([field, extra], axis=1)


def wide_lines(geo, line):
    return [line[:, q * LANES : (q + 1) * LANES] for q in range(geo.breadth // LANES)]


def wide_row(geo, message, sender, row):
    return jnp.concatenate(
        [row_at(message, sender, row + q) for q in range(geo.breadth // LANES)], axis=1
    )


def put_all(ref, row, lines):
    for i, line in enumerate(lines):
        to = (row + i) * LANES
        ref[:, :, to : to + LANES] = jnp.broadcast_to(line[None], (ref.shape[0], 1, LANES))


def put(ref, target, row, lines):
    for i, line in enumerate(lines):
        to = (row + i) * LANES
        ref[target, :, to : to + LANES] = line


def blank(geo):
    return [jnp.zeros((1, LANES), jnp.float32)] * (geo.breadth // LANES)


def matrix(geo, state, top, low, top_wide, above, below):
    breadth = geo.breadth
    width = breadth + LANES
    after = pltpu.roll(top_wide, width - 1, 1)[:, :breadth]
    before = pltpu.roll(top_wide, 1, 1)[:, :breadth]
    line_at = iota((geo.height, breadth), 0)
    down = jnp.where(line_at == geo.height - 1, below, pltpu.roll(low, geo.height - 1, 0))
    up = jnp.where(line_at == 0, above, pltpu.roll(low, 1, 0))
    top_out = state(DIAG_T) * top - state(LINK_R) * after - state(LINK_L) * before - state(VIA) * low
    low_out = state(DIAG_B) * low - state(LINK_D) * down - state(LINK_U) * up - state(VIA) * top
    return top_out, low_out


def links(geo, row, col, wire_ref):
    height, breadth = geo.height, geo.breadth
    line_at = iota((height, breadth), 0)
    col_at = iota((height, breadth), 1)
    right = jnp.where((col == geo.cols - 1) & (col_at == breadth - 1), 0.0, wire_ref[0])
    down = jnp.where((row == geo.rows - 1) & (line_at == height - 1), 0.0, wire_ref[1])
    return right, down


def fetch(pairs, semaphores):
    copies = [
        pltpu.make_async_copy(source, target, semaphores.at[i])
        for i, (source, target) in enumerate(pairs)
    ]
    for copy in copies:
        copy.start()
    return copies


def open_kernel(geo, *refs):
    inputs, wave_ref, send, rel_ref = refs[:12], *refs[12:15]
    volt_ref, package_ref, decap_ref, decap_cond_ref, supply_ref, state_ref, source_ref = refs[15:22]
    map_ref, mask_ref, cond_ref, wire_ref, cap_ref, via_ref, load_ref, semaphores = refs[22:]
    early = (map_ref, mask_ref, cond_ref, volt_ref, wire_ref)
    late = (cap_ref, via_ref, load_ref, decap_ref, decap_cond_ref, supply_ref, package_ref)
    inputs = inputs[:-1] + (inputs[-1].at[: package_ref.shape[0], :],)
    copies = fetch(tuple(zip(inputs, early + late)), semaphores)
    for copy in copies[: len(early)]:
        copy.wait()
    row, col = place()
    me, east, west, south, north = neighbours(geo, row, col)
    height, breadth = geo.height, geo.breadth
    own_level = row * geo.block_rows + iota((height, breadth), 0) // geo.tile_rows
    rel = lax.div(map_ref[...], jnp.int32(BC)) - own_level
    cond = spread(geo, cond_ref, row, col, rel, breadth // LANES)
    weight = mask_ref[...].astype(jnp.float32) * cond
    rel_ref[...] = rel
    top, low = volt_ref[0], volt_ref[1]
    right, down = links(geo, row, col, wire_ref)
    lines, spill = shares(geo, weight * top, rel, col)
    starts = rows_of(geo, FIRST)
    halo = starts["halo"]
    put_all(send, starts["share"], lines + [spill])
    put(send, me, halo, blank(geo))
    put(send, east, halo, [column_line(geo, top, breadth - 1), column_line(geo, right, breadth - 1)])
    put(send, west, halo, [column_line(geo, top, 0)])
    put(send, north, halo, wide_lines(geo, low[:1]))
    put(send, south, halo, wide_lines(geo, low[height - 1 :]))
    put(send, south, starts["deep"], wide_lines(geo, down[height - 1 :]))
    for copy in copies[len(early) : -1]:
        copy.wait()
    via = via_ref[...]
    decap_cond = decap_cond_ref[...]
    frac = decap_cond / (1.0 + decap_cond)
    cap_top, cap_low = cap_ref[0], cap_ref[1]
    state_ref[LINK_R] = right
    state_ref[LINK_D] = down
    state_ref[VIA] = via
    state_ref[WEIGHT] = weight
    state_ref[DIAG_T] = cap_top + right + via + weight
    state_ref[DIAG_B] = cap_low + down + via + frac
    supply = spread(geo, supply_ref, row, col, rel, breadth // LANES)
    source_ref[0] = cap_top * top + weight * supply
    source_ref[1] = cap_low * low + frac * decap_ref[...] - wave_ref[0] * load_ref[...]
    copies[-1].wait()


def first_kernel(
    geo,
    package_in,
    message,
    package_ref,
    volt_ref,
    base_ref,
    source_ref,
    rel_ref,
    send,
    state_ref,
    residual_ref,
    direction_ref,
    package_more_ref,
    sums_ref,
    semaphore,
):
    rows_here = package_ref.shape[0]
    more = pltpu.make_async_copy(
        package_in.at[rows_here : geo.own, :], package_more_ref, semaphore
    )
    more.start()
    row, col = place()
    me, east, west, south, north = neighbours(geo, row, col)
    height, breadth = geo.height, geo.breadth
    starts = rows_of(geo, FIRST)
    halo = starts["halo"]
    gather_shares(geo, message, starts, sums_ref)
    totals = product(geo, package_ref, sums_ref)

    rel = rel_ref[...]
    top, low = volt_ref[0], volt_ref[1]
    planes = {at: base_ref[at] for at in (LINK_R, LINK_D, VIA, WEIGHT)}
    weight, right, down = planes[WEIGHT], planes[LINK_R], planes[LINK_D]
    line_at = iota((height, breadth), 0)
    first_col = iota((height, LANES), 1) == 0
    edge = jnp.where(col > 0, row_at(message, west, halo + 1), 0.0)
    left = pltpu.roll(right, 1, 1)
    left = jnp.concatenate(
        [jnp.where(first_col, line_column(geo, edge), left[:, :LANES]), left[:, LANES:]], axis=1
    )
    edge = jnp.where(row > 0, wide_row(geo, message, north, starts["deep"]), 0.0)
    up = jnp.where(line_at == 0, edge, pltpu.roll(down, 1, 0))
    diag_top = base_ref[DIAG_T] + left
    diag_low = base_ref[DIAG_B] + up
    planes.update(
        {
            LINK_L: left,
            LINK_U: up,
            DIAG_T: diag_top,
            DIAG_B: diag_low,
            INV_T: 1.0 / diag_top,
            INV_B: 1.0 / diag_low,
        }
    )
    for at, plane in planes.items():
        state_ref[at] = plane
    wide = beside(
        geo,
        top,
        row_at(message, east, halo),
        row_at(message, west, halo),
    )
    top_out, low_out = matrix(
        geo,
        planes.__getitem__,
        top,
        low,
        wide,
        wide_row(geo, message, north, halo),
        wide_row(geo, message, south, halo),
    )
    residual_top = source_ref[0] - top_out
    residual_low = source_ref[1] - low_out
    residual_ref[0] = residual_top
    residual_ref[1] = residual_low
    gain = steps_of()[0][1]
    direction_top = gain * residual_top * planes[INV_T]
    direction_low = gain * residual_low * planes[INV_B]
    direction_ref[0] = direction_top
    direction_ref[1] = direction_low
    pull = weight * planes[INV_T]
    lines, spill = shares(geo, weight * direction_top, rel, col)
    square_lines, square_spill = shares(geo, weight * pull, rel, col, 1)
    starts = rows_of(geo, SECOND)
    halo = starts["halo"]
    put_all(send, starts["share"], lines + [spill + square_spill] + square_lines)
    put(send, me, halo, blank(geo))
    below = rel.astype(jnp.float32)
    for target, at in ((east, breadth - 1), (west, 0)):
        both = column_line(geo, pull, at) + column_line(geo, below, at, LANES // 2)
        put(send, target, halo, [column_line(geo, direction_top, at), both])
    put(send, north, halo, wide_lines(geo, direction_low[:1]))
    put(send, south, halo, wide_lines(geo, direction_low[height - 1 :]))
    more.wait()
    totals = totals + product(geo, package_more_ref, sums_ref)
    put_all(send, starts["own"], own_lines(geo, totals, own_start(geo, me)))


def finish_direction(geo, message, product_ref, row, col, stage, direction, pull, rel):
    gain = steps_of()[stage][1]
    coupled = spread(geo, product_ref, row, col, rel, rel.shape[1] // LANES)
    return direction + gain * pull * coupled, coupled


def step_kernel(geo, stage, *refs):
    package_refs, refs = refs[:2], refs[2:]
    if stage == 1:
        (message, state_ref, residual_in, direction_in, iterate_in, rel_ref) = refs[:6]
        (send, residual_ref, direction_ref, iterate_ref, pull_ref, wide_rel_ref, squares_ref) = refs[6:13]
    else:
        (message, state_ref, residual_in, direction_in, iterate_in) = refs[:5]
        (pull_ref, wide_rel_ref, squares_ref) = refs[5:8]
        (send, iterate_ref) = refs[8:10]
        if stage < DEG - 1:
            (residual_ref, direction_ref) = refs[10:12]
    product_ref, sums_ref = refs[-2:]
    row, col = place()
    me, east, west, south, north = neighbours(geo, row, col)
    height, breadth = geo.height, geo.breadth
    gain_before = steps_of()[stage - 1][1]
    starts = rows_of(geo, SECOND if stage == 1 else NEXT)
    halo = starts["halo"]
    gather_own(geo, message, starts, product_ref)
    gather_shares(geo, message, starts, sums_ref)
    if stage == 1:
        gather_shares(geo, message, starts, squares_ref, "square", 1)
    sums_ref[...] = sums_ref[...] + gain_before * squares_ref[...] * product_ref[...]
    own = own_lines(geo, products(geo, package_refs, sums_ref), own_start(geo, me))

    def state(at):
        return state_ref[at]

    weight = state(WEIGHT)
    if stage == 1:
        pull = beside(
            geo,
            weight * state(INV_T),
            row_at(message, east, halo + 1),
            row_at(message, west, halo + 1),
        )
        wide_rel = beside(
            geo,
            rel_ref[...].astype(jnp.float32),
            row_at(message, east, halo + 1),
            row_at(message, west, halo + 1),
            LANES // 2,
        ).astype(jnp.int32)
        pull_ref[...] = pull
        wide_rel_ref[...] = wide_rel
    else:
        pull = pull_ref[...]
        wide_rel = wide_rel_ref[...]
    rel = wide_rel[:, :breadth]
    wide = beside(
        geo,
        direction_in[0],
        row_at(message, east, halo),
        row_at(message, west, halo),
    )
    wide, coupled = finish_direction(
        geo, message, product_ref, row, col, stage - 1, wide, pull, wide_rel
    )
    top = wide[:, :breadth]
    low = direction_in[1]
    top_out, low_out = matrix(
        geo,
        state,
        top,
        low,
        wide,
        wide_row(geo, message, north, halo),
        wide_row(geo, message, south, halo),
    )
    residual_top = residual_in[0] + weight * coupled[:, :breadth] - top_out
    residual_low = residual_in[1] - low_out
    keep, gain = steps_of()[stage]
    direction_top = keep * top + gain * residual_top * state(INV_T)
    direction_low = keep * low + gain * residual_low * state(INV_B)
    iterate_top = iterate_in[0] + top
    iterate_low = iterate_in[1] + low
    if stage == DEG - 1:
        iterate_top = iterate_top + direction_top
        iterate_low = iterate_low + direction_low
        lines, spill = shares(geo, weight * iterate_top, rel, col)
    else:
        residual_ref[0] = residual_top
        residual_ref[1] = residual_low
        direction_ref[0] = direction_top
        direction_ref[1] = direction_low
        lines, spill = shares(geo, weight * direction_top, rel, col)
    iterate_ref[0] = iterate_top
    iterate_ref[1] = iterate_low
    starts = rows_of(geo, NEXT if stage < DEG - 1 else LAST)
    put_all(send, starts["own"], own + lines + [spill])
    if stage < DEG - 1:
        halo = starts["halo"]
        put(send, me, halo, blank(geo))
        put(send, east, halo, [column_line(geo, direction_top, breadth - 1)])
        put(send, west, halo, [column_line(geo, direction_top, 0)])
        put(send, north, halo, wide_lines(geo, direction_low[:1]))
        put(send, south, halo, wide_lines(geo, direction_low[height - 1 :]))


def last_kernel(
    geo,
    package_ref,
    package_more_ref,
    message,
    iterate_ref,
    pull_ref,
    wide_rel_ref,
    squares_ref,
    decap_ref,
    decap_cond_ref,
    supply_ref,
    voltage_ref,
    decap_volt_ref,
    bump_volt_ref,
    product_ref,
    sums_ref,
):
    row, col = place()
    me = row * geo.cols + col
    breadth = geo.breadth
    gain = steps_of()[DEG - 1][1]
    starts = rows_of(geo, LAST)
    gather_own(geo, message, starts, product_ref)
    gather_shares(geo, message, starts, sums_ref)
    sums_ref[...] = sums_ref[...] + gain * squares_ref[...] * product_ref[...]
    own = own_lines(geo, products(geo, (package_ref, package_more_ref), sums_ref), 0)
    if geo.own >= LANES:
        supply = supply_ref[pl.ds(me * len(own), len(own)), :]
        bump_volt_ref[...] = supply + jnp.concatenate(own, axis=0)
    else:
        sharers = LANES // geo.own
        line = jnp.broadcast_to(supply_ref[pl.ds(me // sharers, 1), :], (SUBS, LANES))
        line = lookup(line, (iota((SUBS, LANES), 1) + own_start(geo, me)) % LANES)
        bump_volt_ref[...] = (line[:1] + own[0])[:, : geo.own]
    coupled = spread(
        geo, product_ref, row, col, wide_rel_ref[:, :breadth], breadth // LANES
    )
    low = iterate_ref[1]
    voltage_ref[0] = iterate_ref[0] + gain * pull_ref[:, :breadth] * coupled
    voltage_ref[1] = low
    decap_cond = decap_cond_ref[...]
    decap_volt_ref[...] = (decap_ref[...] + decap_cond * low) / (1.0 + decap_cond)


def exchange(message):
    return lax.all_to_all(message, AXES, split_axis=0, concat_axis=0, tiled=True)


def call(kernel, operands, outputs, scratch=(), outside=(), scalar=None):
    inside = pl.BlockSpec(memory_space=pltpu.VMEM)
    specs = [inside] * len(operands)
    if scalar is not None:
        specs[scalar] = pl.BlockSpec(memory_space=pltpu.SMEM)
    specs = [pl.BlockSpec(memory_space=pltpu.HBM)] * len(outside) + specs
    outside = [pltpu.with_memory_space_constraint(array, pltpu.HBM) for array in outside]
    out_specs = [
        pl.BlockSpec(memory_space=getattr(output, "memory_space", pltpu.VMEM)) for output in outputs
    ]
    return pl.pallas_call(
        kernel,
        out_shape=list(outputs),
        in_specs=specs,
        out_specs=out_specs,
        scratch_shapes=list(scratch),
        compiler_params=pltpu.CompilerParams(vmem_limit_bytes=16 * 2**20),
    )(*outside, *operands)


def shards(
    volt_start,
    cap_dt,
    wire_cond,
    via_cond,
    load_current,
    load_wave,
    decap_state,
    decap_cond,
    bump_map,
    via_mask,
    bump_cond,
    bump_supply,
    package,
):
    height, breadth = via_cond.shape
    rows, cols = lax.axis_size("row"), lax.axis_size("col")
    block_rows, block_cols = BR // rows, BC // cols
    own, lattice = package.shape
    geo = Geometry(
        height,
        breadth,
        rows,
        cols,
        own,
        block_rows,
        block_cols,
        height // block_rows,
        breadth // block_cols,
        lattice,
    )
    devices = rows * cols
    here = own * OPENING // SUBS // SUBS * SUBS
    f32 = jnp.float32
    table = (lattice // LANES, LANES)
    cond = bump_cond.reshape(table)
    supply = bump_supply.reshape(table)
    field = pltpu.VMEM((height, breadth), f32)
    pair = pltpu.VMEM((2, height, breadth), f32)

    def message(parts):
        return pltpu.VMEM((devices, 1, rows_of(geo, parts)["end"] * LANES), f32)

    held = pltpu.VMEM(table, f32)

    whole = pltpu.VMEM((height, breadth), jnp.int32)
    sent, rel, volt, package_here, decap, decap_cond, supply, base, source = call(
        functools.partial(open_kernel, geo),
        (load_wave,),
        (
            message(FIRST),
            whole,
            pair,
            pltpu.VMEM((here, lattice), f32),
            field,
            field,
            held,
            pltpu.VMEM((10, height, breadth), f32),
            pair,
        ),
        (whole, whole, held, pair, pair, field, field, pltpu.SemaphoreType.DMA((12,))),
        outside=(
            bump_map,
            via_mask,
            cond,
            volt_start,
            wire_cond,
            cap_dt,
            via_cond,
            load_current,
            decap_state,
            decap_cond,
            supply,
            package,
        ),
        scalar=0,
    )
    sent, state, residual, direction, package_more = call(
        functools.partial(first_kernel, geo),
        (exchange(sent), package_here, volt, base, source, rel),
        (
            message(SECOND),
            pltpu.VMEM((10, height, breadth), f32),
            pair,
            pair,
            pltpu.VMEM((own - here, lattice), f32),
        ),
        (held, pltpu.SemaphoreType.DMA),
        outside=(package,),
    )
    wide = (height, breadth + LANES)
    sent, residual, direction, iterate, pull, wide_rel, squares = call(
        functools.partial(step_kernel, geo, 1),
        (package_here, package_more, exchange(sent), state, residual, direction, volt, rel),
        (message(NEXT), pair, pair, pair, pltpu.VMEM(wide, f32), pltpu.VMEM(wide, jnp.int32), held),
        (held, held),
    )
    for stage in range(2, DEG):
        sent, iterate, *carried = call(
            functools.partial(step_kernel, geo, stage),
            (
                package_here,
                package_more,
                exchange(sent),
                state,
                residual,
                direction,
                iterate,
                pull,
                wide_rel,
                squares,
            ),
            (message(NEXT), pair, pair, pair) if stage < DEG - 1 else (message(LAST), pair),
            (held, held),
        )
        if carried:
            residual, direction = carried
    voltage, decap_volt, bump_volt = call(
        functools.partial(last_kernel, geo),
        (
            package_here,
            package_more,
            exchange(sent),
            iterate,
            pull,
            wide_rel,
            squares,
            decap,
            decap_cond,
            supply,
        ),
        (
            jax.ShapeDtypeStruct((2, height, breadth), f32),
            jax.ShapeDtypeStruct((height, breadth), f32),
            jax.ShapeDtypeStruct((max(1, own // LANES), min(own, LANES)), f32),
        ),
        (held, held),
    )
    return voltage, decap_volt, bump_volt.reshape(own)


def solution(mesh):
    field = P("row", "col")
    pair = P(None, "row", "col")
    return jax.shard_map(
        shards,
        mesh=mesh,
        in_specs=(
            pair,
            pair,
            pair,
            field,
            field,
            P(),
            field,
            field,
            field,
            field,
            P(),
            P(),
            P(AXES, None),
        ),
        out_specs=(pair, field, P(AXES)),
        check_vma=False,
    )
```

```python
import collections
import functools

import jax
import jax.numpy as jnp
from jax import lax
from jax.experimental import pallas as pl
from jax.experimental.pallas import tpu as pltpu
from jax.sharding import PartitionSpec as P

BR = 128
BC = 64
DEG = 4

CHEB_LO = 0.05
CHEB_HI = 2.0
CHEB_MID = (CHEB_HI + CHEB_LO) / 2.0
CHEB_HALF = (CHEB_HI - CHEB_LO) / 2.0
CHEB_RATIO = CHEB_MID / CHEB_HALF

LANES = 128
SUBS = 8
AXES = ("row", "col")

FIRST = ("share", "spill", "halo", "deep")
SECOND = ("own", "share", "spill", "square", "halo")
NEXT = ("own", "share", "spill", "halo")
LAST = ("own", "share", "spill")

(LINK_R, LINK_L, LINK_D, LINK_U, VIA, WEIGHT, DIAG_T, DIAG_B, INV_T, INV_B) = range(10)

Geometry = collections.namedtuple(
    "Geometry",
    [
        "height",
        "breadth",
        "rows",
        "cols",
        "own",
        "block_rows",
        "block_cols",
        "tile_rows",
        "tile_cols",
        "lattice",
    ],
)


def rows_of(geo, parts):
    sizes = {
        "own": max(1, geo.own // LANES),
        "share": -(-geo.block_rows * geo.block_cols // LANES),
        "square": -(-geo.block_rows * geo.block_cols // LANES),
        "spill": 1,
        "halo": geo.breadth // LANES,
        "deep": geo.breadth // LANES,
    }
    starts, end = {}, 0
    for part in parts:
        starts[part] = end
        end += sizes[part]
    starts["end"] = end
    return starts


def row_at(message, device, row):
    return message[device, :, row * LANES : (row + 1) * LANES]


def steps_of():
    factors = [(0.0, 1.0 / CHEB_MID)]
    rho_now = 1.0 / CHEB_RATIO
    for _ in range(DEG - 1):
        rho_next = 1.0 / (2.0 * CHEB_RATIO - rho_now)
        factors.append((rho_next * rho_now, 2.0 * rho_next / CHEB_HALF))
        rho_now = rho_next
    return factors


def iota(shape, dim):
    return lax.broadcasted_iota(jnp.int32, shape, dim)


def lookup(table, index):
    return jnp.take_along_axis(table, index, axis=1, mode="promise_in_bounds")


def place():
    row = lax.axis_index("row")
    col = lax.axis_index("col")
    return row, col


def neighbours(geo, row, col):
    me = row * geo.cols + col
    east = jnp.where(col < geo.cols - 1, me + 1, me)
    west = jnp.where(col > 0, me - 1, me)
    south = jnp.where(row < geo.rows - 1, me + geo.cols, me)
    north = jnp.where(row > 0, me - geo.cols, me)
    return me, east, west, south, north


def per_band(geo):
    return geo.block_rows * BC // LANES


def spread(geo, ref, row, col, rel, tiles):
    span = per_band(geo)
    base = row * span
    count = geo.lattice // LANES
    lines = [ref[pl.ds(base + t, 1), :] for t in range(span)]
    lines.append(ref[pl.ds(jnp.minimum(base + span, count - 1), 1), :])
    per_line = LANES // BC
    sub = iota((SUBS, LANES), 0)
    lane = iota((SUBS, LANES), 1)
    last = geo.breadth // LANES
    columns = []
    for q in range(tiles):
        if q < last:
            columns.append(col * geo.block_cols + (lane + q * LANES) // geo.tile_cols)
        else:
            after = jnp.minimum((col + 1) * geo.block_cols, BC - 1)
            before = jnp.maximum(col * geo.block_cols - 1, 0)
            columns.append(jnp.where(lane < LANES // 2, after, before))
    bands = []
    for g in range(geo.height // SUBS):
        picks = []
        for shift in (0, 1):
            levels = [(g * SUBS + i) // geo.tile_rows + shift for i in range(SUBS)]
            held = [level // per_line for level in levels]
            table = jnp.broadcast_to(lines[held[0]], (SUBS, LANES))
            for i in range(1, SUBS):
                if held[i] != held[i - 1]:
                    table = jnp.where(
                        sub >= i, jnp.broadcast_to(lines[held[i]], (SUBS, LANES)), table
                    )
            part = ((g * SUBS + sub) // geo.tile_rows + shift) % per_line
            picks.append([lookup(table, part * BC + columns[q]) for q in range(tiles)])
        bands.append(
            jnp.concatenate(
                [
                    jnp.where(
                        rel[g * SUBS : (g + 1) * SUBS, q * LANES : (q + 1) * LANES] == 0,
                        picks[0][q],
                        picks[1][q],
                    )
                    for q in range(tiles)
                ],
                axis=1,
            )
        )
    return jnp.concatenate(bands, axis=0)


def shares(geo, weighted, rel, col, half=0):
    height, breadth = geo.height, geo.breadth
    near = jnp.where(rel == 0, weighted, 0.0)
    both = jnp.concatenate([near, weighted - near], axis=0)
    high = both.astype(jnp.bfloat16)
    rest = both - high.astype(jnp.float32)
    mid = rest.astype(jnp.bfloat16)
    low = (rest - mid.astype(jnp.float32)).astype(jnp.bfloat16)
    adder = (
        iota((breadth, LANES), 0) // geo.tile_cols == iota((breadth, LANES), 1) % geo.block_cols
    )
    adder = adder.astype(jnp.float32).astype(jnp.bfloat16)
    summed = jnp.dot(
        jnp.concatenate([high, mid, low], axis=0), adder, preferred_element_type=jnp.float32
    )
    summed = summed[: 2 * height] + summed[2 * height : 4 * height] + summed[4 * height :]
    sub = iota((SUBS, LANES), 0)
    segment = iota((SUBS, LANES), 1) // geo.block_cols
    segments = LANES // geo.block_cols
    packed = -(-geo.block_rows // segments)
    slot = col + half * (BC // geo.block_cols)
    totals = [jnp.zeros((SUBS, LANES), jnp.float32) for _ in range(packed)]
    spill = jnp.zeros((SUBS, LANES), jnp.float32)
    for shift in (0, 1):
        for g in range(height // SUBS):
            first = g * SUBS // geo.tile_rows + shift
            final = (g * SUBS + SUBS - 1) // geo.tile_rows + shift
            level = (g * SUBS + sub) // geo.tile_rows + shift
            start = shift * height + g * SUBS
            block = summed[start : start + SUBS]
            for h in range(packed):
                if first < (h + 1) * segments and final >= h * segments:
                    hit = level == segment + h * segments
                    if final >= geo.block_rows:
                        hit = hit & (level < geo.block_rows)
                    totals[h] = totals[h] + jnp.where(hit, block, 0.0)
            if final >= geo.block_rows:
                hit = (level == geo.block_rows) & (segment == slot)
                spill = spill + jnp.where(hit, block, 0.0)
    lines = [jnp.sum(total, axis=0, keepdims=True) for total in totals]
    return lines, jnp.sum(spill, axis=0, keepdims=True)


def gather_shares(geo, message, starts, out_ref, part="share", half=0):
    span = per_band(geo)
    per_line = LANES // BC
    segments = LANES // geo.block_cols
    sub = iota((SUBS, LANES), 0)
    lane = iota((SUBS, LANES), 1)
    level = sub * per_line + lane // BC
    index = (level % segments) * geo.block_cols + lane % geo.block_cols
    owner = (lane % BC) // geo.block_cols
    packed = -(-geo.block_rows // segments)

    def band(r):
        total = jnp.zeros((SUBS, LANES), jnp.float32)
        for c in range(geo.cols):
            sender = r * geo.cols + c
            table = jnp.broadcast_to(row_at(message, sender, starts[part]), (SUBS, LANES))
            for h in range(1, packed):
                line = row_at(message, sender, starts[part] + h)
                table = jnp.where(
                    sub >= h * segments // per_line, jnp.broadcast_to(line, (SUBS, LANES)), table
                )
            total = jnp.where(owner == c, lookup(table, index), total)
        return total

    def spill(r):
        line = row_at(message, r * geo.cols, starts["spill"])
        for c in range(1, geo.cols):
            line = line + row_at(message, r * geo.cols + c, starts["spill"])
        line = jnp.broadcast_to(line, (SUBS, LANES))
        if half:
            line = pltpu.roll(line, LANES - half * BC, 1)
        return jnp.where((sub == 0) & (lane < BC), line, 0.0)

    if geo.rows <= 8:
        for r in range(geo.rows):
            total = band(r)
            if r > 0:
                total = total + spill(r - 1)
            out_ref[pl.ds(r * span, span), :] = total[:span]
    else:

        def one(r, carry):
            above = jnp.where(r > 0, spill(jnp.maximum(r - 1, 0)), 0.0)
            out_ref[pl.ds(r * span, span), :] = (band(r) + above)[:span]
            return carry

        lax.fori_loop(0, geo.rows, one, 0)


def gather_own(geo, message, starts, out_ref):
    devices = geo.rows * geo.cols
    if geo.own >= LANES:
        lines = geo.own // LANES
        for d in range(devices):
            for i in range(lines):
                at = d * lines + i
                out_ref[at : at + 1, :] = row_at(message, d, starts["own"] + i)
    else:
        sharers = LANES // geo.own
        for t in range(devices // sharers):
            line = row_at(message, t * sharers, starts["own"])
            for d in range(1, sharers):
                line = line + row_at(message, t * sharers + d, starts["own"])
            out_ref[t : t + 1, :] = line


def product(geo, package_ref, sums_ref):
    groups = geo.own // SUBS
    totals = [jnp.zeros((SUBS, LANES), jnp.float32) for _ in range(groups)]
    for t in range(geo.lattice // LANES):
        line = jnp.broadcast_to(sums_ref[t : t + 1, :], (SUBS, LANES))
        for g in range(groups):
            block = package_ref[g * SUBS : (g + 1) * SUBS, t * LANES : (t + 1) * LANES]
            totals[g] = totals[g] + block * line
    return totals


def own_lines(geo, totals, start):
    per_line = min(len(totals), LANES // SUBS)
    sub = iota((SUBS, LANES), 0)
    lane = iota((SUBS, LANES), 1)
    lines = []
    for h in range(len(totals) // per_line):
        line = jnp.zeros((SUBS, LANES), jnp.float32)
        for q in range(per_line):
            column = jnp.sum(totals[h * per_line + q], axis=1, keepdims=True)
            line = jnp.where(lane == start + q * SUBS + sub, column, line)
        lines.append(jnp.sum(line, axis=0, keepdims=True))
    return lines


def own_start(geo, me):
    if geo.own >= LANES:
        return 0
    return (me % (LANES // geo.own)) * geo.own


def column_line(geo, field, at, start=0):
    sub = iota((SUBS, LANES), 0)
    lane = iota((SUBS, LANES), 1)
    total = jnp.zeros((SUBS, LANES), jnp.float32)
    for g in range(geo.height // SUBS):
        column = jnp.broadcast_to(field[g * SUBS : (g + 1) * SUBS, at : at + 1], (SUBS, LANES))
        total = total + jnp.where(lane == start + g * SUBS + sub, column, 0.0)
    return jnp.sum(total, axis=0, keepdims=True)


def line_column(geo, line, start=0):
    sub = iota((SUBS, LANES), 0)
    table = jnp.broadcast_to(line, (SUBS, LANES))
    return jnp.concatenate(
        [lookup(table, start + g * SUBS + sub) for g in range(geo.height // SUBS)], axis=0
    )


def beside(geo, field, east_line, west_line, start=0):
    lane = iota((geo.height, LANES), 1)
    extra = jnp.where(
        lane == 0,
        line_column(geo, east_line, start),
        jnp.where(lane == LANES - 1, line_column(geo, west_line, start), 0.0),
    )
    return jnp.concatenate([field, extra], axis=1)


def wide_lines(geo, line):
    return [line[:, q * LANES : (q + 1) * LANES] for q in range(geo.breadth // LANES)]


def wide_row(geo, message, sender, row):
    return jnp.concatenate(
        [row_at(message, sender, row + q) for q in range(geo.breadth // LANES)], axis=1
    )


def put_all(ref, row, lines):
    for i, line in enumerate(lines):
        to = (row + i) * LANES
        ref[:, :, to : to + LANES] = jnp.broadcast_to(line[None], (ref.shape[0], 1, LANES))


def put(ref, target, row, lines):
    for i, line in enumerate(lines):
        to = (row + i) * LANES
        ref[target, :, to : to + LANES] = line


def blank(geo):
    return [jnp.zeros((1, LANES), jnp.float32)] * (geo.breadth // LANES)


def matrix(geo, state, top, low, top_wide, above, below):
    breadth = geo.breadth
    width = breadth + LANES
    after = pltpu.roll(top_wide, width - 1, 1)[:, :breadth]
    before = pltpu.roll(top_wide, 1, 1)[:, :breadth]
    line_at = iota((geo.height, breadth), 0)
    down = jnp.where(line_at == geo.height - 1, below, pltpu.roll(low, geo.height - 1, 0))
    up = jnp.where(line_at == 0, above, pltpu.roll(low, 1, 0))
    top_out = state(DIAG_T) * top - state(LINK_R) * after - state(LINK_L) * before - state(VIA) * low
    low_out = state(DIAG_B) * low - state(LINK_D) * down - state(LINK_U) * up - state(VIA) * top
    return top_out, low_out


def links(geo, row, col, wire_ref):
    height, breadth = geo.height, geo.breadth
    line_at = iota((height, breadth), 0)
    col_at = iota((height, breadth), 1)
    right = jnp.where((col == geo.cols - 1) & (col_at == breadth - 1), 0.0, wire_ref[0])
    down = jnp.where((row == geo.rows - 1) & (line_at == height - 1), 0.0, wire_ref[1])
    return right, down


def fetch(pairs, semaphores):
    copies = [
        pltpu.make_async_copy(source, target, semaphores.at[i])
        for i, (source, target) in enumerate(pairs)
    ]
    for copy in copies:
        copy.start()
    return copies


def open_kernel(geo, *refs):
    inputs, wave_ref, send, rel_ref = refs[:12], *refs[12:15]
    volt_ref, package_ref, decap_ref, decap_cond_ref, supply_ref, state_ref, source_ref = refs[15:22]
    map_ref, mask_ref, cond_ref, wire_ref, cap_ref, via_ref, load_ref, semaphores = refs[22:]
    early = (map_ref, mask_ref, cond_ref, volt_ref, wire_ref)
    late = (cap_ref, via_ref, load_ref, decap_ref, decap_cond_ref, supply_ref, package_ref)
    copies = fetch(tuple(zip(inputs, early + late)), semaphores)
    for copy in copies[: len(early)]:
        copy.wait()
    row, col = place()
    me, east, west, south, north = neighbours(geo, row, col)
    height, breadth = geo.height, geo.breadth
    own_level = row * geo.block_rows + iota((height, breadth), 0) // geo.tile_rows
    rel = lax.div(map_ref[...], jnp.int32(BC)) - own_level
    cond = spread(geo, cond_ref, row, col, rel, breadth // LANES)
    weight = mask_ref[...].astype(jnp.float32) * cond
    rel_ref[...] = rel
    top, low = volt_ref[0], volt_ref[1]
    right, down = links(geo, row, col, wire_ref)
    lines, spill = shares(geo, weight * top, rel, col)
    starts = rows_of(geo, FIRST)
    halo = starts["halo"]
    put_all(send, starts["share"], lines + [spill])
    put(send, me, halo, blank(geo))
    put(send, east, halo, [column_line(geo, top, breadth - 1), column_line(geo, right, breadth - 1)])
    put(send, west, halo, [column_line(geo, top, 0)])
    put(send, north, halo, wide_lines(geo, low[:1]))
    put(send, south, halo, wide_lines(geo, low[height - 1 :]))
    put(send, south, starts["deep"], wide_lines(geo, down[height - 1 :]))
    for copy in copies[len(early) : -1]:
        copy.wait()
    via = via_ref[...]
    decap_cond = decap_cond_ref[...]
    frac = decap_cond / (1.0 + decap_cond)
    cap_top, cap_low = cap_ref[0], cap_ref[1]
    state_ref[LINK_R] = right
    state_ref[LINK_D] = down
    state_ref[VIA] = via
    state_ref[WEIGHT] = weight
    state_ref[DIAG_T] = cap_top + right + via + weight
    state_ref[DIAG_B] = cap_low + down + via + frac
    supply = spread(geo, supply_ref, row, col, rel, breadth // LANES)
    source_ref[0] = cap_top * top + weight * supply
    source_ref[1] = cap_low * low + frac * decap_ref[...] - wave_ref[0] * load_ref[...]
    copies[-1].wait()


def first_kernel(
    geo,
    message,
    package_ref,
    volt_ref,
    base_ref,
    source_ref,
    rel_ref,
    send,
    state_ref,
    residual_ref,
    direction_ref,
    sums_ref,
):
    row, col = place()
    me, east, west, south, north = neighbours(geo, row, col)
    height, breadth = geo.height, geo.breadth
    starts = rows_of(geo, FIRST)
    halo = starts["halo"]
    gather_shares(geo, message, starts, sums_ref)

    rel = rel_ref[...]
    top, low = volt_ref[0], volt_ref[1]
    planes = {at: base_ref[at] for at in (LINK_R, LINK_D, VIA, WEIGHT)}
    weight, right, down = planes[WEIGHT], planes[LINK_R], planes[LINK_D]
    line_at = iota((height, breadth), 0)
    first_col = iota((height, LANES), 1) == 0
    edge = jnp.where(col > 0, row_at(message, west, halo + 1), 0.0)
    left = pltpu.roll(right, 1, 1)
    left = jnp.concatenate(
        [jnp.where(first_col, line_column(geo, edge), left[:, :LANES]), left[:, LANES:]], axis=1
    )
    edge = jnp.where(row > 0, wide_row(geo, message, north, starts["deep"]), 0.0)
    up = jnp.where(line_at == 0, edge, pltpu.roll(down, 1, 0))
    diag_top = base_ref[DIAG_T] + left
    diag_low = base_ref[DIAG_B] + up
    planes.update(
        {
            LINK_L: left,
            LINK_U: up,
            DIAG_T: diag_top,
            DIAG_B: diag_low,
            INV_T: 1.0 / diag_top,
            INV_B: 1.0 / diag_low,
        }
    )
    for at, plane in planes.items():
        state_ref[at] = plane
    wide = beside(
        geo,
        top,
        row_at(message, east, halo),
        row_at(message, west, halo),
    )
    top_out, low_out = matrix(
        geo,
        planes.__getitem__,
        top,
        low,
        wide,
        wide_row(geo, message, north, halo),
        wide_row(geo, message, south, halo),
    )
    residual_top = source_ref[0] - top_out
    residual_low = source_ref[1] - low_out
    residual_ref[0] = residual_top
    residual_ref[1] = residual_low
    gain = steps_of()[0][1]
    direction_top = gain * residual_top * planes[INV_T]
    direction_low = gain * residual_low * planes[INV_B]
    direction_ref[0] = direction_top
    direction_ref[1] = direction_low
    pull = weight * planes[INV_T]
    lines, spill = shares(geo, weight * direction_top, rel, col)
    square_lines, square_spill = shares(geo, weight * pull, rel, col, 1)
    starts = rows_of(geo, SECOND)
    halo = starts["halo"]
    put_all(send, starts["share"], lines + [spill + square_spill] + square_lines)
    put(send, me, halo, blank(geo))
    below = rel.astype(jnp.float32)
    for target, at in ((east, breadth - 1), (west, 0)):
        both = column_line(geo, pull, at) + column_line(geo, below, at, LANES // 2)
        put(send, target, halo, [column_line(geo, direction_top, at), both])
    put(send, north, halo, wide_lines(geo, direction_low[:1]))
    put(send, south, halo, wide_lines(geo, direction_low[height - 1 :]))
    own = own_lines(geo, product(geo, package_ref, sums_ref), own_start(geo, me))
    put_all(send, starts["own"], own)


def finish_direction(geo, message, product_ref, row, col, stage, direction, pull, rel):
    gain = steps_of()[stage][1]
    coupled = spread(geo, product_ref, row, col, rel, rel.shape[1] // LANES)
    return direction + gain * pull * coupled, coupled


def step_kernel(geo, stage, *refs):
    if stage == 1:
        (message, package_ref, state_ref, residual_in, direction_in, iterate_in, rel_ref) = refs[:7]
        (send, residual_ref, direction_ref, iterate_ref, pull_ref, wide_rel_ref, squares_ref) = refs[7:14]
    else:
        (message, package_ref, state_ref, residual_in, direction_in, iterate_in) = refs[:6]
        (pull_ref, wide_rel_ref, squares_ref) = refs[6:9]
        (send, iterate_ref) = refs[9:11]
        if stage < DEG - 1:
            (residual_ref, direction_ref) = refs[11:13]
    product_ref, sums_ref = refs[-2:]
    row, col = place()
    me, east, west, south, north = neighbours(geo, row, col)
    height, breadth = geo.height, geo.breadth
    gain_before = steps_of()[stage - 1][1]
    starts = rows_of(geo, SECOND if stage == 1 else NEXT)
    halo = starts["halo"]
    gather_own(geo, message, starts, product_ref)
    gather_shares(geo, message, starts, sums_ref)
    if stage == 1:
        gather_shares(geo, message, starts, squares_ref, "square", 1)
    sums_ref[...] = sums_ref[...] + gain_before * squares_ref[...] * product_ref[...]

    def state(at):
        return state_ref[at]

    weight = state(WEIGHT)
    if stage == 1:
        pull = beside(
            geo,
            weight * state(INV_T),
            row_at(message, east, halo + 1),
            row_at(message, west, halo + 1),
        )
        wide_rel = beside(
            geo,
            rel_ref[...].astype(jnp.float32),
            row_at(message, east, halo + 1),
            row_at(message, west, halo + 1),
            LANES // 2,
        ).astype(jnp.int32)
        pull_ref[...] = pull
        wide_rel_ref[...] = wide_rel
    else:
        pull = pull_ref[...]
        wide_rel = wide_rel_ref[...]
    rel = wide_rel[:, :breadth]
    wide = beside(
        geo,
        direction_in[0],
        row_at(message, east, halo),
        row_at(message, west, halo),
    )
    wide, coupled = finish_direction(
        geo, message, product_ref, row, col, stage - 1, wide, pull, wide_rel
    )
    top = wide[:, :breadth]
    low = direction_in[1]
    top_out, low_out = matrix(
        geo,
        state,
        top,
        low,
        wide,
        wide_row(geo, message, north, halo),
        wide_row(geo, message, south, halo),
    )
    residual_top = residual_in[0] + weight * coupled[:, :breadth] - top_out
    residual_low = residual_in[1] - low_out
    keep, gain = steps_of()[stage]
    direction_top = keep * top + gain * residual_top * state(INV_T)
    direction_low = keep * low + gain * residual_low * state(INV_B)
    iterate_top = iterate_in[0] + top
    iterate_low = iterate_in[1] + low
    if stage == DEG - 1:
        iterate_top = iterate_top + direction_top
        iterate_low = iterate_low + direction_low
        lines, spill = shares(geo, weight * iterate_top, rel, col)
    else:
        residual_ref[0] = residual_top
        residual_ref[1] = residual_low
        direction_ref[0] = direction_top
        direction_ref[1] = direction_low
        lines, spill = shares(geo, weight * direction_top, rel, col)
    iterate_ref[0] = iterate_top
    iterate_ref[1] = iterate_low
    starts = rows_of(geo, NEXT if stage < DEG - 1 else LAST)
    put_all(send, starts["share"], lines + [spill])
    if stage < DEG - 1:
        halo = starts["halo"]
        put(send, me, halo, blank(geo))
        put(send, east, halo, [column_line(geo, direction_top, breadth - 1)])
        put(send, west, halo, [column_line(geo, direction_top, 0)])
        put(send, north, halo, wide_lines(geo, direction_low[:1]))
        put(send, south, halo, wide_lines(geo, direction_low[height - 1 :]))
    own = own_lines(geo, product(geo, package_ref, sums_ref), own_start(geo, me))
    put_all(send, starts["own"], own)


def last_kernel(
    geo,
    message,
    package_ref,
    iterate_ref,
    pull_ref,
    wide_rel_ref,
    squares_ref,
    decap_ref,
    decap_cond_ref,
    supply_ref,
    voltage_ref,
    decap_volt_ref,
    bump_volt_ref,
    product_ref,
    sums_ref,
):
    row, col = place()
    me = row * geo.cols + col
    breadth = geo.breadth
    gain = steps_of()[DEG - 1][1]
    starts = rows_of(geo, LAST)
    gather_own(geo, message, starts, product_ref)
    gather_shares(geo, message, starts, sums_ref)
    sums_ref[...] = sums_ref[...] + gain * squares_ref[...] * product_ref[...]
    own = own_lines(geo, product(geo, package_ref, sums_ref), 0)
    if geo.own >= LANES:
        supply = supply_ref[pl.ds(me * len(own), len(own)), :]
        bump_volt_ref[...] = supply + jnp.concatenate(own, axis=0)
    else:
        sharers = LANES // geo.own
        line = jnp.broadcast_to(supply_ref[pl.ds(me // sharers, 1), :], (SUBS, LANES))
        line = lookup(line, (iota((SUBS, LANES), 1) + own_start(geo, me)) % LANES)
        bump_volt_ref[...] = (line[:1] + own[0])[:, : geo.own]
    coupled = spread(
        geo, product_ref, row, col, wide_rel_ref[:, :breadth], breadth // LANES
    )
    low = iterate_ref[1]
    voltage_ref[0] = iterate_ref[0] + gain * pull_ref[:, :breadth] * coupled
    voltage_ref[1] = low
    decap_cond = decap_cond_ref[...]
    decap_volt_ref[...] = (decap_ref[...] + decap_cond * low) / (1.0 + decap_cond)


def exchange(message):
    return lax.all_to_all(message, AXES, split_axis=0, concat_axis=0, tiled=True)


def call(kernel, operands, outputs, scratch=(), outside=(), scalar=None):
    inside = pl.BlockSpec(memory_space=pltpu.VMEM)
    specs = [inside] * len(operands)
    if scalar is not None:
        specs[scalar] = pl.BlockSpec(memory_space=pltpu.SMEM)
    specs = [pl.BlockSpec(memory_space=pltpu.HBM)] * len(outside) + specs
    outside = [pltpu.with_memory_space_constraint(array, pltpu.HBM) for array in outside]
    out_specs = [
        pl.BlockSpec(memory_space=getattr(output, "memory_space", pltpu.VMEM)) for output in outputs
    ]
    return pl.pallas_call(
        kernel,
        out_shape=list(outputs),
        in_specs=specs,
        out_specs=out_specs,
        scratch_shapes=list(scratch),
        compiler_params=pltpu.CompilerParams(vmem_limit_bytes=16 * 2**20),
    )(*outside, *operands)


def shards(
    volt_start,
    cap_dt,
    wire_cond,
    via_cond,
    load_current,
    load_wave,
    decap_state,
    decap_cond,
    bump_map,
    via_mask,
    bump_cond,
    bump_supply,
    package,
):
    height, breadth = via_cond.shape
    rows, cols = lax.axis_size("row"), lax.axis_size("col")
    block_rows, block_cols = BR // rows, BC // cols
    own, lattice = package.shape
    geo = Geometry(
        height,
        breadth,
        rows,
        cols,
        own,
        block_rows,
        block_cols,
        height // block_rows,
        breadth // block_cols,
        lattice,
    )
    devices = rows * cols
    f32 = jnp.float32
    table = (lattice // LANES, LANES)
    cond = bump_cond.reshape(table)
    supply = bump_supply.reshape(table)
    field = pltpu.VMEM((height, breadth), f32)
    pair = pltpu.VMEM((2, height, breadth), f32)

    def message(parts):
        return pltpu.VMEM((devices, 1, rows_of(geo, parts)["end"] * LANES), f32)

    held = pltpu.VMEM(table, f32)

    whole = pltpu.VMEM((height, breadth), jnp.int32)
    sent, rel, volt, package, decap, decap_cond, supply, base, source = call(
        functools.partial(open_kernel, geo),
        (load_wave,),
        (
            message(FIRST),
            whole,
            pair,
            pltpu.VMEM(package.shape, f32),
            field,
            field,
            held,
            pltpu.VMEM((10, height, breadth), f32),
            pair,
        ),
        (whole, whole, held, pair, pair, field, field, pltpu.SemaphoreType.DMA((12,))),
        outside=(
            bump_map,
            via_mask,
            cond,
            volt_start,
            wire_cond,
            cap_dt,
            via_cond,
            load_current,
            decap_state,
            decap_cond,
            supply,
            package,
        ),
        scalar=0,
    )
    sent, state, residual, direction = call(
        functools.partial(first_kernel, geo),
        (exchange(sent), package, volt, base, source, rel),
        (
            message(SECOND),
            pltpu.VMEM((10, height, breadth), f32),
            pair,
            pair,
        ),
        (held,),
    )
    wide = (height, breadth + LANES)
    sent, residual, direction, iterate, pull, wide_rel, squares = call(
        functools.partial(step_kernel, geo, 1),
        (exchange(sent), package, state, residual, direction, volt, rel),
        (message(NEXT), pair, pair, pair, pltpu.VMEM(wide, f32), pltpu.VMEM(wide, jnp.int32), held),
        (held, held),
    )
    for stage in range(2, DEG):
        sent, iterate, *carried = call(
            functools.partial(step_kernel, geo, stage),
            (
                exchange(sent),
                package,
                state,
                residual,
                direction,
                iterate,
                pull,
                wide_rel,
                squares,
            ),
            (message(NEXT), pair, pair, pair) if stage < DEG - 1 else (message(LAST), pair),
            (held, held),
        )
        if carried:
            residual, direction = carried
    voltage, decap_volt, bump_volt = call(
        functools.partial(last_kernel, geo),
        (
            exchange(sent),
            package,
            iterate,
            pull,
            wide_rel,
            squares,
            decap,
            decap_cond,
            supply,
        ),
        (
            jax.ShapeDtypeStruct((2, height, breadth), f32),
            jax.ShapeDtypeStruct((height, breadth), f32),
            jax.ShapeDtypeStruct((max(1, own // LANES), min(own, LANES)), f32),
        ),
        (held, held),
    )
    return voltage, decap_volt, bump_volt.reshape(own)


def solution(mesh):
    field = P("row", "col")
    pair = P(None, "row", "col")
    return jax.shard_map(
        shards,
        mesh=mesh,
        in_specs=(
            pair,
            pair,
            pair,
            field,
            field,
            P(),
            field,
            field,
            field,
            field,
            P(),
            P(),
            P(AXES, None),
        ),
        out_specs=(pair, field, P(AXES)),
        check_vma=False,
    )
```

```python
import collections
import functools

import jax
import jax.numpy as jnp
from jax import lax
from jax.experimental import pallas as pl
from jax.experimental.pallas import tpu as pltpu
from jax.sharding import PartitionSpec as P

BR = 128
BC = 64
DEG = 4

CHEB_LO = 0.05
CHEB_HI = 2.0
CHEB_MID = (CHEB_HI + CHEB_LO) / 2.0
CHEB_HALF = (CHEB_HI - CHEB_LO) / 2.0
CHEB_RATIO = CHEB_MID / CHEB_HALF

LANES = 128
SUBS = 8
AXES = ("row", "col")

FIRST = ("share", "spill", "halo", "deep")
SECOND = ("own", "share", "spill", "square", "halo")
NEXT = ("own", "share", "spill", "halo")
LAST = ("own", "share", "spill")

(LINK_R, LINK_L, LINK_D, LINK_U, VIA, WEIGHT, DIAG_T, DIAG_B, INV_T, INV_B) = range(10)

Geometry = collections.namedtuple(
    "Geometry",
    [
        "height",
        "breadth",
        "rows",
        "cols",
        "own",
        "block_rows",
        "block_cols",
        "tile_rows",
        "tile_cols",
        "lattice",
    ],
)


def rows_of(geo, parts):
    sizes = {
        "own": max(1, geo.own // LANES),
        "share": -(-geo.block_rows * geo.block_cols // LANES),
        "square": -(-geo.block_rows * geo.block_cols // LANES),
        "spill": 1,
        "halo": geo.breadth // LANES,
        "deep": geo.breadth // LANES,
    }
    starts, end = {}, 0
    for part in parts:
        starts[part] = end
        end += sizes[part]
    starts["end"] = end
    return starts


def row_at(message, device, row):
    return message[device, :, row * LANES : (row + 1) * LANES]


def steps_of():
    factors = [(0.0, 1.0 / CHEB_MID)]
    rho_now = 1.0 / CHEB_RATIO
    for _ in range(DEG - 1):
        rho_next = 1.0 / (2.0 * CHEB_RATIO - rho_now)
        factors.append((rho_next * rho_now, 2.0 * rho_next / CHEB_HALF))
        rho_now = rho_next
    return factors


def iota(shape, dim):
    return lax.broadcasted_iota(jnp.int32, shape, dim)


def lookup(table, index):
    return jnp.take_along_axis(table, index, axis=1, mode="promise_in_bounds")


def place():
    row = lax.axis_index("row")
    col = lax.axis_index("col")
    return row, col


def neighbours(geo, row, col):
    me = row * geo.cols + col
    east = jnp.where(col < geo.cols - 1, me + 1, me)
    west = jnp.where(col > 0, me - 1, me)
    south = jnp.where(row < geo.rows - 1, me + geo.cols, me)
    north = jnp.where(row > 0, me - geo.cols, me)
    return me, east, west, south, north


def per_band(geo):
    return geo.block_rows * BC // LANES


def spread(geo, ref, row, col, rel, tiles):
    span = per_band(geo)
    base = row * span
    count = geo.lattice // LANES
    lines = [ref[pl.ds(base + t, 1), :] for t in range(span)]
    lines.append(ref[pl.ds(jnp.minimum(base + span, count - 1), 1), :])
    per_line = LANES // BC
    sub = iota((SUBS, LANES), 0)
    lane = iota((SUBS, LANES), 1)
    last = geo.breadth // LANES
    columns = []
    for q in range(tiles):
        if q < last:
            columns.append(col * geo.block_cols + (lane + q * LANES) // geo.tile_cols)
        else:
            after = jnp.minimum((col + 1) * geo.block_cols, BC - 1)
            before = jnp.maximum(col * geo.block_cols - 1, 0)
            columns.append(jnp.where(lane < LANES // 2, after, before))
    bands = []
    for g in range(geo.height // SUBS):
        picks = []
        for shift in (0, 1):
            levels = [(g * SUBS + i) // geo.tile_rows + shift for i in range(SUBS)]
            held = [level // per_line for level in levels]
            table = jnp.broadcast_to(lines[held[0]], (SUBS, LANES))
            for i in range(1, SUBS):
                if held[i] != held[i - 1]:
                    table = jnp.where(
                        sub >= i, jnp.broadcast_to(lines[held[i]], (SUBS, LANES)), table
                    )
            part = ((g * SUBS + sub) // geo.tile_rows + shift) % per_line
            picks.append([lookup(table, part * BC + columns[q]) for q in range(tiles)])
        bands.append(
            jnp.concatenate(
                [
                    jnp.where(
                        rel[g * SUBS : (g + 1) * SUBS, q * LANES : (q + 1) * LANES] == 0,
                        picks[0][q],
                        picks[1][q],
                    )
                    for q in range(tiles)
                ],
                axis=1,
            )
        )
    return jnp.concatenate(bands, axis=0)


def shares(geo, weighted, rel, col, half=0):
    height, breadth = geo.height, geo.breadth
    near = jnp.where(rel == 0, weighted, 0.0)
    both = jnp.concatenate([near, weighted - near], axis=0)
    high = both.astype(jnp.bfloat16)
    rest = both - high.astype(jnp.float32)
    mid = rest.astype(jnp.bfloat16)
    low = (rest - mid.astype(jnp.float32)).astype(jnp.bfloat16)
    adder = (
        iota((breadth, LANES), 0) // geo.tile_cols == iota((breadth, LANES), 1) % geo.block_cols
    )
    adder = adder.astype(jnp.float32).astype(jnp.bfloat16)
    summed = jnp.dot(
        jnp.concatenate([high, mid, low], axis=0), adder, preferred_element_type=jnp.float32
    )
    summed = summed[: 2 * height] + summed[2 * height : 4 * height] + summed[4 * height :]
    sub = iota((SUBS, LANES), 0)
    segment = iota((SUBS, LANES), 1) // geo.block_cols
    segments = LANES // geo.block_cols
    packed = -(-geo.block_rows // segments)
    slot = col + half * (BC // geo.block_cols)
    totals = [jnp.zeros((SUBS, LANES), jnp.float32) for _ in range(packed)]
    spill = jnp.zeros((SUBS, LANES), jnp.float32)
    for shift in (0, 1):
        for g in range(height // SUBS):
            first = g * SUBS // geo.tile_rows + shift
            final = (g * SUBS + SUBS - 1) // geo.tile_rows + shift
            level = (g * SUBS + sub) // geo.tile_rows + shift
            start = shift * height + g * SUBS
            block = summed[start : start + SUBS]
            for h in range(packed):
                if first < (h + 1) * segments and final >= h * segments:
                    hit = level == segment + h * segments
                    if final >= geo.block_rows:
                        hit = hit & (level < geo.block_rows)
                    totals[h] = totals[h] + jnp.where(hit, block, 0.0)
            if final >= geo.block_rows:
                hit = (level == geo.block_rows) & (segment == slot)
                spill = spill + jnp.where(hit, block, 0.0)
    lines = [jnp.sum(total, axis=0, keepdims=True) for total in totals]
    return lines, jnp.sum(spill, axis=0, keepdims=True)


def gather_shares(geo, message, starts, out_ref, part="share", half=0):
    span = per_band(geo)
    per_line = LANES // BC
    segments = LANES // geo.block_cols
    sub = iota((SUBS, LANES), 0)
    lane = iota((SUBS, LANES), 1)
    level = sub * per_line + lane // BC
    index = (level % segments) * geo.block_cols + lane % geo.block_cols
    owner = (lane % BC) // geo.block_cols
    packed = -(-geo.block_rows // segments)

    def band(r):
        total = jnp.zeros((SUBS, LANES), jnp.float32)
        for c in range(geo.cols):
            sender = r * geo.cols + c
            table = jnp.broadcast_to(row_at(message, sender, starts[part]), (SUBS, LANES))
            for h in range(1, packed):
                line = row_at(message, sender, starts[part] + h)
                table = jnp.where(
                    sub >= h * segments // per_line, jnp.broadcast_to(line, (SUBS, LANES)), table
                )
            total = jnp.where(owner == c, lookup(table, index), total)
        return total

    def spill(r):
        line = row_at(message, r * geo.cols, starts["spill"])
        for c in range(1, geo.cols):
            line = line + row_at(message, r * geo.cols + c, starts["spill"])
        line = jnp.broadcast_to(line, (SUBS, LANES))
        if half:
            line = pltpu.roll(line, LANES - half * BC, 1)
        return jnp.where((sub == 0) & (lane < BC), line, 0.0)

    if geo.rows <= 8:
        for r in range(geo.rows):
            total = band(r)
            if r > 0:
                total = total + spill(r - 1)
            out_ref[pl.ds(r * span, span), :] = total[:span]
    else:

        def one(r, carry):
            above = jnp.where(r > 0, spill(jnp.maximum(r - 1, 0)), 0.0)
            out_ref[pl.ds(r * span, span), :] = (band(r) + above)[:span]
            return carry

        lax.fori_loop(0, geo.rows, one, 0)


def gather_own(geo, message, starts, out_ref):
    devices = geo.rows * geo.cols
    if geo.own >= LANES:
        lines = geo.own // LANES
        for d in range(devices):
            for i in range(lines):
                at = d * lines + i
                out_ref[at : at + 1, :] = row_at(message, d, starts["own"] + i)
    else:
        sharers = LANES // geo.own
        for t in range(devices // sharers):
            line = row_at(message, t * sharers, starts["own"])
            for d in range(1, sharers):
                line = line + row_at(message, t * sharers + d, starts["own"])
            out_ref[t : t + 1, :] = line


def product(geo, package_ref, sums_ref):
    groups = geo.own // SUBS
    totals = [jnp.zeros((SUBS, LANES), jnp.float32) for _ in range(groups)]
    for t in range(geo.lattice // LANES):
        line = jnp.broadcast_to(sums_ref[t : t + 1, :], (SUBS, LANES))
        for g in range(groups):
            block = package_ref[g * SUBS : (g + 1) * SUBS, t * LANES : (t + 1) * LANES]
            totals[g] = totals[g] + block * line
    return totals


def own_lines(geo, totals, start):
    per_line = min(len(totals), LANES // SUBS)
    sub = iota((SUBS, LANES), 0)
    lane = iota((SUBS, LANES), 1)
    lines = []
    for h in range(len(totals) // per_line):
        line = jnp.zeros((SUBS, LANES), jnp.float32)
        for q in range(per_line):
            column = jnp.sum(totals[h * per_line + q], axis=1, keepdims=True)
            line = jnp.where(lane == start + q * SUBS + sub, column, line)
        lines.append(jnp.sum(line, axis=0, keepdims=True))
    return lines


def own_start(geo, me):
    if geo.own >= LANES:
        return 0
    return (me % (LANES // geo.own)) * geo.own


def column_line(geo, field, at, start=0):
    sub = iota((SUBS, LANES), 0)
    lane = iota((SUBS, LANES), 1)
    total = jnp.zeros((SUBS, LANES), jnp.float32)
    for g in range(geo.height // SUBS):
        column = jnp.broadcast_to(field[g * SUBS : (g + 1) * SUBS, at : at + 1], (SUBS, LANES))
        total = total + jnp.where(lane == start + g * SUBS + sub, column, 0.0)
    return jnp.sum(total, axis=0, keepdims=True)


def line_column(geo, line, start=0):
    sub = iota((SUBS, LANES), 0)
    table = jnp.broadcast_to(line, (SUBS, LANES))
    return jnp.concatenate(
        [lookup(table, start + g * SUBS + sub) for g in range(geo.height // SUBS)], axis=0
    )


def beside(geo, field, east_line, west_line, start=0):
    lane = iota((geo.height, LANES), 1)
    extra = jnp.where(
        lane == 0,
        line_column(geo, east_line, start),
        jnp.where(lane == LANES - 1, line_column(geo, west_line, start), 0.0),
    )
    return jnp.concatenate([field, extra], axis=1)


def wide_lines(geo, line):
    return [line[:, q * LANES : (q + 1) * LANES] for q in range(geo.breadth // LANES)]


def wide_row(geo, message, sender, row):
    return jnp.concatenate(
        [row_at(message, sender, row + q) for q in range(geo.breadth // LANES)], axis=1
    )


def put_all(ref, row, lines):
    for i, line in enumerate(lines):
        to = (row + i) * LANES
        ref[:, :, to : to + LANES] = jnp.broadcast_to(line[None], (ref.shape[0], 1, LANES))


def put(ref, target, row, lines):
    for i, line in enumerate(lines):
        to = (row + i) * LANES
        ref[target, :, to : to + LANES] = line


def blank(geo):
    return [jnp.zeros((1, LANES), jnp.float32)] * (geo.breadth // LANES)


def matrix(geo, state, top, low, top_wide, above, below):
    breadth = geo.breadth
    width = breadth + LANES
    after = pltpu.roll(top_wide, width - 1, 1)[:, :breadth]
    before = pltpu.roll(top_wide, 1, 1)[:, :breadth]
    line_at = iota((geo.height, breadth), 0)
    down = jnp.where(line_at == geo.height - 1, below, pltpu.roll(low, geo.height - 1, 0))
    up = jnp.where(line_at == 0, above, pltpu.roll(low, 1, 0))
    top_out = state(DIAG_T) * top - state(LINK_R) * after - state(LINK_L) * before - state(VIA) * low
    low_out = state(DIAG_B) * low - state(LINK_D) * down - state(LINK_U) * up - state(VIA) * top
    return top_out, low_out


def links(geo, row, col, wire_ref):
    height, breadth = geo.height, geo.breadth
    line_at = iota((height, breadth), 0)
    col_at = iota((height, breadth), 1)
    right = jnp.where((col == geo.cols - 1) & (col_at == breadth - 1), 0.0, wire_ref[0])
    down = jnp.where((row == geo.rows - 1) & (line_at == height - 1), 0.0, wire_ref[1])
    return right, down


def fetch(pairs, semaphores):
    copies = [
        pltpu.make_async_copy(source, target, semaphores.at[i])
        for i, (source, target) in enumerate(pairs)
    ]
    for copy in copies:
        copy.start()
    return copies


def open_kernel(geo, *refs):
    inputs, wave_ref, send, rel_ref = refs[:12], *refs[12:15]
    volt_ref, package_ref, decap_ref, decap_cond_ref, supply_ref, state_ref, source_ref = refs[15:22]
    map_ref, mask_ref, cond_ref, wire_ref, cap_ref, via_ref, load_ref, semaphores = refs[22:]
    early = (map_ref, mask_ref, cond_ref, volt_ref, wire_ref)
    late = (cap_ref, via_ref, load_ref, decap_ref, decap_cond_ref, supply_ref, package_ref)
    copies = fetch(tuple(zip(inputs, early + late)), semaphores)
    for copy in copies[: len(early)]:
        copy.wait()
    row, col = place()
    me, east, west, south, north = neighbours(geo, row, col)
    height, breadth = geo.height, geo.breadth
    own_level = row * geo.block_rows + iota((height, breadth), 0) // geo.tile_rows
    rel = lax.div(map_ref[...], jnp.int32(BC)) - own_level
    cond = spread(geo, cond_ref, row, col, rel, breadth // LANES)
    weight = mask_ref[...].astype(jnp.float32) * cond
    rel_ref[...] = rel
    top, low = volt_ref[0], volt_ref[1]
    right, down = links(geo, row, col, wire_ref)
    lines, spill = shares(geo, weight * top, rel, col)
    starts = rows_of(geo, FIRST)
    halo = starts["halo"]
    put_all(send, starts["share"], lines + [spill])
    put(send, me, halo, blank(geo))
    put(send, east, halo, [column_line(geo, top, breadth - 1), column_line(geo, right, breadth - 1)])
    put(send, west, halo, [column_line(geo, top, 0)])
    put(send, north, halo, wide_lines(geo, low[:1]))
    put(send, south, halo, wide_lines(geo, low[height - 1 :]))
    put(send, south, starts["deep"], wide_lines(geo, down[height - 1 :]))
    for copy in copies[len(early) : -1]:
        copy.wait()
    via = via_ref[...]
    decap_cond = decap_cond_ref[...]
    frac = decap_cond / (1.0 + decap_cond)
    cap_top, cap_low = cap_ref[0], cap_ref[1]
    state_ref[LINK_R] = right
    state_ref[LINK_D] = down
    state_ref[VIA] = via
    state_ref[WEIGHT] = weight
    state_ref[DIAG_T] = cap_top + right + via + weight
    state_ref[DIAG_B] = cap_low + down + via + frac
    supply = spread(geo, supply_ref, row, col, rel, breadth // LANES)
    source_ref[0] = cap_top * top + weight * supply
    source_ref[1] = cap_low * low + frac * decap_ref[...] - wave_ref[0] * load_ref[...]
    copies[-1].wait()


def first_kernel(
    geo,
    message,
    package_ref,
    volt_ref,
    base_ref,
    source_ref,
    rel_ref,
    send,
    state_ref,
    residual_ref,
    direction_ref,
    sums_ref,
):
    row, col = place()
    me, east, west, south, north = neighbours(geo, row, col)
    height, breadth = geo.height, geo.breadth
    starts = rows_of(geo, FIRST)
    halo = starts["halo"]
    gather_shares(geo, message, starts, sums_ref)

    rel = rel_ref[...]
    top, low = volt_ref[0], volt_ref[1]
    planes = {at: base_ref[at] for at in (LINK_R, LINK_D, VIA, WEIGHT)}
    weight, right, down = planes[WEIGHT], planes[LINK_R], planes[LINK_D]
    line_at = iota((height, breadth), 0)
    first_col = iota((height, LANES), 1) == 0
    edge = jnp.where(col > 0, row_at(message, west, halo + 1), 0.0)
    left = pltpu.roll(right, 1, 1)
    left = jnp.concatenate(
        [jnp.where(first_col, line_column(geo, edge), left[:, :LANES]), left[:, LANES:]], axis=1
    )
    edge = jnp.where(row > 0, wide_row(geo, message, north, starts["deep"]), 0.0)
    up = jnp.where(line_at == 0, edge, pltpu.roll(down, 1, 0))
    diag_top = base_ref[DIAG_T] + left
    diag_low = base_ref[DIAG_B] + up
    planes.update(
        {
            LINK_L: left,
            LINK_U: up,
            DIAG_T: diag_top,
            DIAG_B: diag_low,
            INV_T: 1.0 / diag_top,
            INV_B: 1.0 / diag_low,
        }
    )
    for at, plane in planes.items():
        state_ref[at] = plane
    wide = beside(
        geo,
        top,
        row_at(message, east, halo),
        row_at(message, west, halo),
    )
    top_out, low_out = matrix(
        geo,
        planes.__getitem__,
        top,
        low,
        wide,
        wide_row(geo, message, north, halo),
        wide_row(geo, message, south, halo),
    )
    residual_top = source_ref[0] - top_out
    residual_low = source_ref[1] - low_out
    residual_ref[0] = residual_top
    residual_ref[1] = residual_low
    gain = steps_of()[0][1]
    direction_top = gain * residual_top * planes[INV_T]
    direction_low = gain * residual_low * planes[INV_B]
    direction_ref[0] = direction_top
    direction_ref[1] = direction_low
    pull = weight * planes[INV_T]
    lines, spill = shares(geo, weight * direction_top, rel, col)
    square_lines, square_spill = shares(geo, weight * pull, rel, col, 1)
    starts = rows_of(geo, SECOND)
    halo = starts["halo"]
    put_all(send, starts["share"], lines + [spill + square_spill] + square_lines)
    put(send, me, halo, blank(geo))
    below = rel.astype(jnp.float32)
    for target, at in ((east, breadth - 1), (west, 0)):
        both = column_line(geo, pull, at) + column_line(geo, below, at, LANES // 2)
        put(send, target, halo, [column_line(geo, direction_top, at), both])
    put(send, north, halo, wide_lines(geo, direction_low[:1]))
    put(send, south, halo, wide_lines(geo, direction_low[height - 1 :]))
    own = own_lines(geo, product(geo, package_ref, sums_ref), own_start(geo, me))
    put_all(send, starts["own"], own)


def finish_direction(geo, message, product_ref, row, col, stage, direction, pull, rel):
    gain = steps_of()[stage][1]
    coupled = spread(geo, product_ref, row, col, rel, rel.shape[1] // LANES)
    return direction + gain * pull * coupled, coupled


def step_kernel(geo, stage, *refs):
    if stage == 1:
        (message, package_ref, state_ref, residual_in, direction_in, iterate_in, rel_ref) = refs[:7]
        (send, residual_ref, direction_ref, iterate_ref, pull_ref, wide_rel_ref, squares_ref) = refs[7:14]
    else:
        (message, package_ref, state_ref, residual_in, direction_in, iterate_in) = refs[:6]
        (pull_ref, wide_rel_ref, squares_ref) = refs[6:9]
        (send, iterate_ref) = refs[9:11]
        if stage < DEG - 1:
            (residual_ref, direction_ref) = refs[11:13]
    product_ref, sums_ref = refs[-2:]
    row, col = place()
    me, east, west, south, north = neighbours(geo, row, col)
    height, breadth = geo.height, geo.breadth
    gain_before = steps_of()[stage - 1][1]
    starts = rows_of(geo, SECOND if stage == 1 else NEXT)
    halo = starts["halo"]
    gather_own(geo, message, starts, product_ref)
    gather_shares(geo, message, starts, sums_ref)
    if stage == 1:
        gather_shares(geo, message, starts, squares_ref, "square", 1)
    sums_ref[...] = sums_ref[...] + gain_before * squares_ref[...] * product_ref[...]

    def state(at):
        return state_ref[at]

    weight = state(WEIGHT)
    if stage == 1:
        pull = beside(
            geo,
            weight * state(INV_T),
            row_at(message, east, halo + 1),
            row_at(message, west, halo + 1),
        )
        wide_rel = beside(
            geo,
            rel_ref[...].astype(jnp.float32),
            row_at(message, east, halo + 1),
            row_at(message, west, halo + 1),
            LANES // 2,
        ).astype(jnp.int32)
        pull_ref[...] = pull
        wide_rel_ref[...] = wide_rel
    else:
        pull = pull_ref[...]
        wide_rel = wide_rel_ref[...]
    rel = wide_rel[:, :breadth]
    wide = beside(
        geo,
        direction_in[0],
        row_at(message, east, halo),
        row_at(message, west, halo),
    )
    wide, coupled = finish_direction(
        geo, message, product_ref, row, col, stage - 1, wide, pull, wide_rel
    )
    top = wide[:, :breadth]
    low = direction_in[1]
    top_out, low_out = matrix(
        geo,
        state,
        top,
        low,
        wide,
        wide_row(geo, message, north, halo),
        wide_row(geo, message, south, halo),
    )
    residual_top = residual_in[0] + weight * coupled[:, :breadth] - top_out
    residual_low = residual_in[1] - low_out
    keep, gain = steps_of()[stage]
    direction_top = keep * top + gain * residual_top * state(INV_T)
    direction_low = keep * low + gain * residual_low * state(INV_B)
    iterate_top = iterate_in[0] + top
    iterate_low = iterate_in[1] + low
    if stage == DEG - 1:
        iterate_top = iterate_top + direction_top
        iterate_low = iterate_low + direction_low
        lines, spill = shares(geo, weight * iterate_top, rel, col)
    else:
        residual_ref[0] = residual_top
        residual_ref[1] = residual_low
        direction_ref[0] = direction_top
        direction_ref[1] = direction_low
        lines, spill = shares(geo, weight * direction_top, rel, col)
    iterate_ref[0] = iterate_top
    iterate_ref[1] = iterate_low
    starts = rows_of(geo, NEXT if stage < DEG - 1 else LAST)
    put_all(send, starts["share"], lines + [spill])
    if stage < DEG - 1:
        halo = starts["halo"]
        put(send, me, halo, blank(geo))
        put(send, east, halo, [column_line(geo, direction_top, breadth - 1)])
        put(send, west, halo, [column_line(geo, direction_top, 0)])
        put(send, north, halo, wide_lines(geo, direction_low[:1]))
        put(send, south, halo, wide_lines(geo, direction_low[height - 1 :]))
    own = own_lines(geo, product(geo, package_ref, sums_ref), own_start(geo, me))
    put_all(send, starts["own"], own)


def last_kernel(
    geo,
    message,
    package_ref,
    iterate_ref,
    pull_ref,
    wide_rel_ref,
    squares_ref,
    decap_ref,
    decap_cond_ref,
    supply_ref,
    voltage_ref,
    decap_volt_ref,
    bump_volt_ref,
    product_ref,
    sums_ref,
):
    row, col = place()
    me = row * geo.cols + col
    breadth = geo.breadth
    gain = steps_of()[DEG - 1][1]
    starts = rows_of(geo, LAST)
    gather_own(geo, message, starts, product_ref)
    gather_shares(geo, message, starts, sums_ref)
    sums_ref[...] = sums_ref[...] + gain * squares_ref[...] * product_ref[...]
    coupled = spread(
        geo, product_ref, row, col, wide_rel_ref[:, :breadth], breadth // LANES
    )
    low = iterate_ref[1]
    voltage_ref[0] = iterate_ref[0] + gain * pull_ref[:, :breadth] * coupled
    voltage_ref[1] = low
    decap_cond = decap_cond_ref[...]
    decap_volt_ref[...] = (decap_ref[...] + decap_cond * low) / (1.0 + decap_cond)
    own = own_lines(geo, product(geo, package_ref, sums_ref), 0)
    if geo.own >= LANES:
        supply = supply_ref[pl.ds(me * len(own), len(own)), :]
        bump_volt_ref[...] = supply + jnp.concatenate(own, axis=0)
    else:
        sharers = LANES // geo.own
        line = jnp.broadcast_to(supply_ref[pl.ds(me // sharers, 1), :], (SUBS, LANES))
        line = lookup(line, (iota((SUBS, LANES), 1) + own_start(geo, me)) % LANES)
        bump_volt_ref[...] = (line[:1] + own[0])[:, : geo.own]


def exchange(message):
    return lax.all_to_all(message, AXES, split_axis=0, concat_axis=0, tiled=True)


def call(kernel, operands, outputs, scratch=(), outside=(), scalar=None):
    inside = pl.BlockSpec(memory_space=pltpu.VMEM)
    specs = [inside] * len(operands)
    if scalar is not None:
        specs[scalar] = pl.BlockSpec(memory_space=pltpu.SMEM)
    specs = [pl.BlockSpec(memory_space=pltpu.HBM)] * len(outside) + specs
    outside = [pltpu.with_memory_space_constraint(array, pltpu.HBM) for array in outside]
    out_specs = [
        pl.BlockSpec(memory_space=getattr(output, "memory_space", pltpu.VMEM)) for output in outputs
    ]
    return pl.pallas_call(
        kernel,
        out_shape=list(outputs),
        in_specs=specs,
        out_specs=out_specs,
        scratch_shapes=list(scratch),
        compiler_params=pltpu.CompilerParams(vmem_limit_bytes=16 * 2**20),
    )(*outside, *operands)


def shards(
    volt_start,
    cap_dt,
    wire_cond,
    via_cond,
    load_current,
    load_wave,
    decap_state,
    decap_cond,
    bump_map,
    via_mask,
    bump_cond,
    bump_supply,
    package,
):
    height, breadth = via_cond.shape
    rows, cols = lax.axis_size("row"), lax.axis_size("col")
    block_rows, block_cols = BR // rows, BC // cols
    own, lattice = package.shape
    geo = Geometry(
        height,
        breadth,
        rows,
        cols,
        own,
        block_rows,
        block_cols,
        height // block_rows,
        breadth // block_cols,
        lattice,
    )
    devices = rows * cols
    f32 = jnp.float32
    table = (lattice // LANES, LANES)
    cond = bump_cond.reshape(table)
    supply = bump_supply.reshape(table)
    field = pltpu.VMEM((height, breadth), f32)
    pair = pltpu.VMEM((2, height, breadth), f32)

    def message(parts):
        return pltpu.VMEM((devices, 1, rows_of(geo, parts)["end"] * LANES), f32)

    held = pltpu.VMEM(table, f32)

    whole = pltpu.VMEM((height, breadth), jnp.int32)
    sent, rel, volt, package, decap, decap_cond, supply, base, source = call(
        functools.partial(open_kernel, geo),
        (load_wave,),
        (
            message(FIRST),
            whole,
            pair,
            pltpu.VMEM(package.shape, f32),
            field,
            field,
            held,
            pltpu.VMEM((10, height, breadth), f32),
            pair,
        ),
        (whole, whole, held, pair, pair, field, field, pltpu.SemaphoreType.DMA((12,))),
        outside=(
            bump_map,
            via_mask,
            cond,
            volt_start,
            wire_cond,
            cap_dt,
            via_cond,
            load_current,
            decap_state,
            decap_cond,
            supply,
            package,
        ),
        scalar=0,
    )
    sent, state, residual, direction = call(
        functools.partial(first_kernel, geo),
        (exchange(sent), package, volt, base, source, rel),
        (
            message(SECOND),
            pltpu.VMEM((10, height, breadth), f32),
            pair,
            pair,
        ),
        (held,),
    )
    wide = (height, breadth + LANES)
    sent, residual, direction, iterate, pull, wide_rel, squares = call(
        functools.partial(step_kernel, geo, 1),
        (exchange(sent), package, state, residual, direction, volt, rel),
        (message(NEXT), pair, pair, pair, pltpu.VMEM(wide, f32), pltpu.VMEM(wide, jnp.int32), held),
        (held, held),
    )
    for stage in range(2, DEG):
        sent, iterate, *carried = call(
            functools.partial(step_kernel, geo, stage),
            (
                exchange(sent),
                package,
                state,
                residual,
                direction,
                iterate,
                pull,
                wide_rel,
                squares,
            ),
            (message(NEXT), pair, pair, pair) if stage < DEG - 1 else (message(LAST), pair),
            (held, held),
        )
        if carried:
            residual, direction = carried
    voltage, decap_volt, bump_volt = call(
        functools.partial(last_kernel, geo),
        (
            exchange(sent),
            package,
            iterate,
            pull,
            wide_rel,
            squares,
            decap,
            decap_cond,
            supply,
        ),
        (
            jax.ShapeDtypeStruct((2, height, breadth), f32),
            jax.ShapeDtypeStruct((height, breadth), f32),
            jax.ShapeDtypeStruct((max(1, own // LANES), min(own, LANES)), f32),
        ),
        (held, held),
    )
    return voltage, decap_volt, bump_volt.reshape(own)


def solution(mesh):
    field = P("row", "col")
    pair = P(None, "row", "col")
    return jax.shard_map(
        shards,
        mesh=mesh,
        in_specs=(
            pair,
            pair,
            pair,
            field,
            field,
            P(),
            field,
            field,
            field,
            field,
            P(),
            P(),
            P(AXES, None),
        ),
        out_specs=(pair, field, P(AXES)),
        check_vma=False,
    )
```
